32 devices in a mesh: section: 4 (over z), space: 8 (over y, x, core).
Axes of the slice: x: 2, y: 2, z: 4, core: 2. Of those that a mesh axis runs over, the one named last changes fastest.
Arguments:
- features: bfloat16 [4, 32, 784, 256], P('section', 'space')
- tissue: int32 [4, 32], P('section'), may hold values from 0 to 1, as said below
- first_weight: bfloat16 [256, 512], replicated, may hold values from -0.375 to 0.375
- first_gain: float32 [512], replicated, may hold values from 0.1 to 1.9
- first_bias: float32 [512], replicated, may hold values from -3 to 3
- second_weight: bfloat16 [512, 1024], P(None, 'space'), may hold values from -0.25 to 0.25
- second_gain: float32 [1024], replicated, may hold values from 0.1 to 1.9
- second_bias: float32 [1024], replicated, may hold values from -3 to 3
Outputs:
- output: bfloat16 [4, 1024, 25088], P('section', 'space')
- first_mean: float32 [512], replicated
- first_var: float32 [512], replicated
- second_mean: float32 [1024], P('space')
- second_var: float32 [1024], P('space')
The draws below stay inside these ranges and needn't reach their ends.
Inputs may be any that keep to these rules, and one draw needn't show every extreme that they name: Every tile row holds at least one tissue tile and at least one tile without tissue.
All inputs are finite; a program needn't handle non-finite values.
Results may differ from the reference program's by a relative error of at most 0.0053.
Values may be sent and summed in bfloat16 or wider, within the bound.
A program may use at most 128 MiB of HBM per device.

```python
import jax
import jax.numpy as jnp
from jax import lax

C1 = 256
C2 = 512
C3 = 1024
PIX = 784
MB = 4
TILES = 32


def draw_features(key, part):
    key_tile, key_chan, key_base = jax.random.split(key, 3)
    positions = jnp.arange(TILES).astype(jnp.float32) / max(TILES - 1, 1)
    tile_scale = jnp.power(10.0, positions)[None, :] * jnp.exp(jax.random.uniform(key_tile, (MB, TILES), jnp.float32, -0.35, 0.35))
    chan_scale = jnp.exp(jax.random.uniform(key_chan, (C1,), jnp.float32, -1.15, 1.15))
    base = jax.random.normal(key_base, (MB, TILES, PIX, C1), jnp.float32)
    values = base * tile_scale[:, :, None, None] * chan_scale
    return values.astype(jnp.bfloat16)


def draw_tissue(key, part):
    key_center, key_width, key_coin = jax.random.split(key, 3)
    center = jax.random.randint(key_center, (MB, 1), TILES // 5, 4 * TILES // 5 + 1)
    width = jax.random.randint(key_width, (MB, 1), TILES // 8 + 1, TILES // 3 + 1)
    places = jnp.arange(TILES)[None, :]
    coin = jax.random.randint(key_coin, (MB, TILES), 0, 10)
    inside = jnp.abs(places - center) < width
    mask = jnp.where(inside, (coin < 9).astype(jnp.int32), (coin < 1).astype(jnp.int32))
    mask = jnp.where(places == center, 1, mask)
    mask = jnp.where(places == (center + TILES // 2) % TILES, 0, mask)
    return mask.astype(jnp.int32)


def steps_of(stream_key, dims, cuts, least, high):
    def one(position, shards_of):
        heights = jax.random.uniform(jax.random.fold_in(jax.random.fold_in(stream_key, 6), position), (shards_of,), jnp.float32, least / len(cuts), high / len(cuts))
        return jnp.repeat(jnp.exp(heights), dims[position] // shards_of).reshape((-1,) + (1,) * (len(dims) - position - 1))

    level = one(*cuts[0])
    for cut in cuts[1:]:
        level = level * one(*cut)
    return level


def noise(key, extent, scale, limit, pieces=(), kind=jnp.bfloat16):
    drawn = scale * jax.random.normal(key, extent, jnp.float32)
    if pieces:
        drawn = drawn * steps_of(key, extent, pieces, -0.22, 0.18)
    return jnp.clip(drawn, -limit, limit).astype(kind)


def setup_inputs(seed: int = 0) -> dict:
    keys = jax.random.split(jax.random.key(seed), 9)
    return {
        "features": draw_features(jax.random.fold_in(keys[8], 71), 0),
        "tissue": draw_tissue(jax.random.fold_in(keys[8], 71), 0),
        "first_weight": noise(keys[2], (C1, C2), C1 ** -0.5, 0.375),
        "first_gain": jnp.clip(1.0 + 0.18 * jax.random.normal(keys[3], (C2,), jnp.float32), 0.1, 1.9),
        "first_bias": noise(keys[4], (C2,), 0.5, 3.0, (), jnp.float32),
        "second_weight": noise(keys[5], (C2, C3), C2 ** -0.5, 0.25, ((1, 8),)),
        "second_gain": jnp.clip(1.0 + 0.18 * jax.random.normal(keys[6], (C3,), jnp.float32), 0.1, 1.9),
        "second_bias": noise(keys[7], (C3,), 0.5, 3.0, (), jnp.float32),
    }


EPS = 1e-05

def statistics(values, weight, count):
    mean_val = lax.optimization_barrier(jnp.sum(values * weight, axis=(0, 1, 2))) / count
    centred = values - mean_val
    var_val = lax.optimization_barrier(jnp.sum(weight * centred * centred, axis=(0, 1, 2))) / count
    return (mean_val, var_val)

def normalize(values, mean_val, var_val, gain, bias):
    return jnp.maximum(gain * (values - mean_val) * lax.rsqrt(var_val + EPS) + bias, 0.0)

def reference(features, tissue, first_weight, first_gain, first_bias, second_weight, second_gain, second_bias):
    weight = tissue.astype(jnp.float32)[:, :, None, None]
    count = jnp.sum(tissue).astype(jnp.float32) * PIX
    first = jnp.einsum('mtpc,cd->mtpd', features.astype(jnp.float32), first_weight.astype(jnp.float32), precision=lax.Precision.HIGHEST)
    first_mean, first_var = statistics(first, weight, count)
    activation = normalize(first, first_mean, first_var, first_gain, first_bias).astype(jnp.bfloat16)
    second = jnp.einsum('mtpc,cd->mtpd', activation.astype(jnp.float32), second_weight.astype(jnp.float32), precision=lax.Precision.HIGHEST)
    second_mean, second_var = statistics(second, weight, count)
    output = normalize(second, second_mean, second_var, second_gain, second_bias).astype(jnp.bfloat16)
    output = jnp.transpose(output, (0, 3, 1, 2)).reshape(MB, C3, TILES * PIX)
    return (output, first_mean, first_var, second_mean, second_var)
```

```python
import functools

import jax
import jax.numpy as jnp
from jax import lax
from jax.experimental import pallas as pl
from jax.experimental.pallas import tpu as pltpu
from jax.sharding import PartitionSpec as P

EPS = 1e-05
MESH = pl.DeviceIdType.MESH


def normalize(values, mean_val, var_val, gain, bias):
    return jnp.maximum(gain * (values - mean_val) * lax.rsqrt(var_val + EPS) + bias, 0.0)


def masked_sum(values, weight):
    return jnp.sum(values * weight, axis=(0, 1, 2))


def channel_first(values):
    batch, tiles_here, pixels, chans = values.shape
    return jnp.transpose(values, (0, 3, 1, 2)).reshape(batch, chans, tiles_here * pixels)


def plain_shards(
    features, tissue, first_weight, first_gain, first_bias, second_weight, second_gain, second_bias
):
    index = lax.axis_index("space")
    tiles_here = features.shape[1]
    pixels = features.shape[2]
    row_mask = tissue[0].astype(jnp.float32)
    own_mask = lax.dynamic_slice_in_dim(row_mask, index * tiles_here, tiles_here)
    own_weight = own_mask[None, :, None, None]
    local_count = jnp.sum(own_mask) * pixels
    first = jnp.einsum("mtpc,cd->mtpd", features, first_weight, preferred_element_type=jnp.float32)
    total, squares, count = lax.psum(
        (
            masked_sum(first, own_weight),
            jnp.sum(first * first * own_weight, axis=(0, 1, 2)),
            local_count,
        ),
        ("section", "space"),
    )
    first_mean = total / count
    first_var = squares / count - first_mean * first_mean
    activation = normalize(first, first_mean, first_var, first_gain, first_bias).astype(
        jnp.bfloat16
    )
    second = jnp.einsum(
        "mtpc,cd->mtpd",
        activation,
        lax.all_gather(second_weight, "space", axis=1, tiled=True),
        preferred_element_type=jnp.float32,
    )
    width_here = second_weight.shape[1]
    moved = lax.all_to_all(channel_first(second), "space", split_axis=1, concat_axis=2, tiled=True)
    row_weight = jnp.repeat(row_mask, pixels)[None, None, :]
    total_two, squares_two = lax.psum(
        (
            jnp.sum(moved * row_weight, axis=(0, 2)),
            jnp.sum(moved * moved * row_weight, axis=(0, 2)),
        ),
        "section",
    )
    second_mean = total_two / count
    second_var = squares_two / count - second_mean * second_mean
    gain_here = lax.dynamic_slice_in_dim(second_gain, index * width_here, width_here)
    bias_here = lax.dynamic_slice_in_dim(second_bias, index * width_here, width_here)
    output = normalize(
        moved, second_mean[:, None], second_var[:, None], gain_here[:, None], bias_here[:, None]
    ).astype(jnp.bfloat16)
    return (output, first_mean, first_var, second_mean, second_var)


def gather_kernel(
    shape,
    tissue,
    x_ref,
    w1,
    g1,
    b1,
    w2,
    second_ref,
    stats1_ref,
    stats2_ref,
    rows_all,
    stage,
    acc,
    coef,
    st1,
    st2,
    st3,
    local_sem,
    stage_sem,
    send_a,
    send_b,
    send_p,
    send_f,
    recv_d,
    recv_p,
    st1_send,
    st1_recv,
    st2_send,
    st2_recv,
    st3_send,
    st3_recv,
):
    n, ns, units, unit, tiles_here, pixels = shape
    block = units * unit
    chunk = 2 * unit
    macros = (units + 1) // 2
    tiles_chip = 2 * tiles_here
    sec = lax.axis_index("section")
    me = lax.axis_index("space")
    core = lax.rem(me, 2)
    cx = lax.rem(me // 2, 2)
    cy = me // 4

    def chip_at(fx, fy):
        return lax.rem(cy + fy, 2) * 2 + lax.rem(cx + fx, 2)

    chip_b = chip_at(core, 1 - core)
    chip_a = chip_at(1 - core, core)
    chip_d = chip_at(1, 1)
    chip_o = chip_at(0, 0)
    dev_a = chip_a * 2 + core
    dev_b = chip_b * 2 + core
    partner = chip_o * 2 + (1 - core)

    def rows_of(chip, kind, k):
        start = (chip * 2 + kind) * block + lax.rem(k + kind, units) * unit
        return rows_all.at[pl.ds(pl.multiple_of(start, unit), unit)]

    def remote(src, dst, send, recv, device):
        return pltpu.make_async_remote_copy(
            src_ref=src, dst_ref=dst, send_sem=send, recv_sem=recv,
            device_id=(sec, device), device_id_type=MESH,
        )

    def own_src(k):
        start = lax.rem(k + core, units) * unit
        return x_ref.at[pl.ds(pl.multiple_of(start, unit), unit)]

    def own_copies(k):
        dst = rows_of(chip_o, core, k)
        return (
            remote(own_src(k), dst, send_a.at[k], recv_d.at[1, k], dev_a),
            remote(own_src(k), dst, send_b.at[k], recv_d.at[0, k], dev_b),
            remote(own_src(k), dst, send_p.at[0, k], recv_p.at[0, k], partner),
        )

    def start_own(k):
        for copy in own_copies(k):
            copy.start()

    def relay(group, chip, k):
        piece = rows_of(chip, core, k)
        return remote(piece, piece, send_p.at[group, k], recv_p.at[group, k], partner)

    def forward(k):
        piece = rows_of(chip_b, core, k)
        return remote(piece, piece, send_f.at[k], recv_d.at[2, k], dev_a)

    barrier = pltpu.get_barrier_semaphore()
    for step in range(1, n):
        pl.semaphore_signal(
            barrier, inc=1, device_id=(sec, lax.rem(me + step, n)), device_id_type=MESH
        )
    for step in range(1, ns):
        pl.semaphore_signal(
            barrier, inc=1, device_id=(lax.rem(sec + step, ns), me), device_id_type=MESH
        )
    own = pltpu.make_async_copy(
        x_ref, rows_all.at[pl.ds(pl.multiple_of(me * block, block), block)], local_sem
    )
    own.start()
    pl.semaphore_wait(barrier, n - 1 + ns - 1)
    start_own(0)
    own.wait()

    def tile_sums(t, carry):
        total, squares, count = carry
        weight = tissue[0, me * tiles_here + t].astype(jnp.float32)
        start = pl.multiple_of(me * block + t * pixels, 16)
        first = jnp.dot(
            rows_all[pl.ds(start, pixels), :], w1[...], preferred_element_type=jnp.float32
        )
        total += weight * jnp.sum(first, axis=0, keepdims=True)
        squares += weight * jnp.sum(first * first, axis=0, keepdims=True)
        return total, squares, count + weight * pixels

    wide = w1.shape[1]
    zero = jnp.zeros((1, wide), jnp.float32)
    total, squares, count = lax.fori_loop(0, tiles_here, tile_sums, (zero, zero, zero))
    mine = st1.at[me]
    mine[0:1, :] = total
    mine[1:2, :] = squares
    mine[2:3, :] = count
    mine[3:8, :] = jnp.zeros((5, wide), jnp.float32)

    def exchange(buf, slot, count_of, send, recv, device_of):
        copies = []
        for step in range(1, count_of):
            other = lax.rem(slot + step, count_of)
            copy = pltpu.make_async_remote_copy(
                src_ref=buf.at[slot], dst_ref=buf.at[slot],
                send_sem=send.at[step], recv_sem=recv.at[slot],
                device_id=device_of(other), device_id_type=MESH,
            )
            copy.start()
            copies.append((copy, other))
        return copies

    def collect(buf, copies, recv, send, device_of):
        for copy, other in copies:
            copy.wait_send()
        for step, (copy, other) in enumerate(copies):
            pltpu.make_async_remote_copy(
                src_ref=buf.at[other], dst_ref=buf.at[other],
                send_sem=send.at[step + 1], recv_sem=recv.at[other],
                device_id=device_of(other), device_id_type=MESH,
            ).wait_recv()

    def in_space(other):
        return (sec, other)

    def in_section(other):
        return (other, me)

    copies = exchange(st1, me, n, st1_send, st1_recv, in_space)
    lax.fori_loop(1, units, lambda k, c: (start_own(k), c)[1], 0)
    collect(st1, copies, st1_recv, st1_send, in_space)
    st2[sec] = jnp.sum(st1[...], axis=0)
    copies = exchange(st2, sec, ns, st2_send, st2_recv, in_section)
    collect(st2, copies, st2_recv, st2_send, in_section)
    sums = jnp.sum(st2[...], axis=0)
    count = sums[2:3, :]
    mean = sums[0:1, :] / count
    var = sums[1:2, :] / count - mean * mean
    scale = g1[...] * lax.rsqrt(var + EPS)
    stats1_ref[0:1, :] = mean
    stats1_ref[1:2, :] = var
    stats1_ref[2:8, :] = jnp.zeros((6, wide), jnp.float32)
    coef[0:1, :] = scale
    coef[1:2, :] = b1[...] - mean * scale
    coef[2:3, :] = count

    acc[...] = jnp.zeros_like(acc)

    def write_out(slot, start):
        return pltpu.make_async_copy(
            stage.at[slot], second_ref.at[:, pl.ds(start, chunk)], stage_sem.at[slot]
        )

    def compute(chip, j, slot):
        base = chip * (2 * block) + j * chunk
        rows = rows_all[pl.ds(pl.multiple_of(base, chunk), chunk), :]
        first = jnp.dot(rows, w1[...], preferred_element_type=jnp.float32)
        act = jnp.maximum(first * coef[0:1, :] + coef[1:2, :], 0.0).astype(jnp.bfloat16)
        second = jnp.dot(act, w2[...], preferred_element_type=jnp.float32).T
        lane = lax.broadcasted_iota(jnp.int32, (1, chunk), 1)
        tile = (j * chunk) // pixels
        mask = jnp.zeros((1, chunk), jnp.float32)
        for i in range(chunk // pixels + 2):
            at = tile + i
            held = tissue[0, chip * tiles_chip + lax.rem(at, tiles_chip)].astype(jnp.float32)
            low = at * pixels - j * chunk
            mask = jnp.where((lane >= low) & (lane < low + pixels), held, mask)
        kept = second * mask
        square = kept * second
        part = acc[0]
        part2 = acc[1]
        for i in range(chunk // 128):
            part += kept[:, i * 128:(i + 1) * 128]
            part2 += square[:, i * 128:(i + 1) * 128]
        acc[0] = part
        acc[1] = part2
        stage[slot] = second
        write_out(slot, pl.multiple_of(base, chunk)).start()

    def compute_macro(chip, m, pending):
        for i in range(2):
            def go(i=i):
                @pl.when(pending(i))
                def _():
                    write_out(i, 0).wait()
                compute(chip, m + macros * i, i)
            if i == 0:
                go()
            else:
                pl.when(m < macros - 1)(go)

    def incoming(kind, chip, group, k):
        piece = rows_of(chip, kind, k)
        if group == "relay":
            return lambda g: remote(
                piece, piece, send_p.at[g, k], recv_p.at[g, k], partner
            ).wait_recv()
        return lambda g: remote(
            piece, piece, send_f.at[k], recv_d.at[g, k], dev_a
        ).wait_recv()

    def each_unit(m, fn):
        fn(2 * m)

        @pl.when(m < macros - 1)
        def _():
            fn(2 * m + 1)

    def own_step(m, c):
        each_unit(m, lambda k: incoming(1 - core, chip_o, "relay", k)(0))
        compute_macro(chip_o, m, lambda i: m >= 1)
        return c

    def side_step(t, c):
        s = lax.rem(t, 2)
        m = t // 2
        chip = chip_at(lax.rem(core + s, 2), lax.rem(1 - core + s, 2))
        group = 1 + lax.rem(core + 1 + s, 2)

        def pass_b(k):
            incoming(core, chip_b, "direct", k)(0)
            forward(k).start()
            relay(2 - core, chip_b, k).start()

        def pass_a(k):
            incoming(core, chip_a, "direct", k)(1)
            relay(1 + core, chip_a, k).start()

        @pl.when(s == 0)
        def _():
            each_unit(m, pass_b)
            each_unit(m, pass_a)

        each_unit(m, lambda k: incoming(1 - core, chip, "relay", k)(group))
        compute_macro(chip, m, lambda i: t >= 0)
        return c

    def last_step(m, c):
        def pass_on(k):
            incoming(core, chip_d, "direct", k)(2)
            relay(3, chip_d, k).start()

        each_unit(m, pass_on)
        each_unit(m, lambda k: incoming(1 - core, chip_d, "relay", k)(3))
        compute_macro(chip_d, m, lambda i: m >= 0)
        return c

    lax.fori_loop(0, macros, own_step, 0)
    lax.fori_loop(0, 2 * macros, side_step, 0)
    lax.fori_loop(0, macros, last_step, 0)

    width = w2.shape[1]
    mine = st3.at[sec]
    mine[0:1, :] = jnp.sum(acc[0].T, axis=0, keepdims=True)
    mine[1:2, :] = jnp.sum(acc[1].T, axis=0, keepdims=True)
    mine[2:8, :] = jnp.zeros((6, width), jnp.float32)
    copies = exchange(st3, sec, ns, st3_send, st3_recv, in_section)

    def drain(k, c):
        for copy in own_copies(k):
            copy.wait_send()
        relay(1, chip_b, k).wait_send()
        relay(2, chip_a, k).wait_send()
        relay(3, chip_d, k).wait_send()
        forward(k).wait_send()
        return c

    lax.fori_loop(0, units, drain, 0)
    for slot in range(2):
        write_out(slot, 0).wait()
    collect(st3, copies, st3_recv, st3_send, in_section)
    sums = jnp.sum(st3[...], axis=0)
    count = coef[2:3, 0:width]
    mean = sums[0:1, :] / count
    stats2_ref[0:1, :] = mean
    stats2_ref[1:2, :] = sums[1:2, :] / count - mean * mean
    stats2_ref[2:8, :] = jnp.zeros((6, width), jnp.float32)


def finish_kernel(stats, gain, bias, second, out):
    scale = gain[...] * lax.rsqrt(stats[1:2, :] + EPS)
    shift = bias[...] - stats[0:1, :] * scale
    size = scale.shape[1]
    scale = jnp.broadcast_to(scale, (size, size)).T[:, 0:1]
    shift = jnp.broadcast_to(shift, (size, size)).T[:, 0:1]
    out[...] = jnp.maximum(second[...] * scale + shift, 0.0).astype(out.dtype)


def units_of(block):
    for units in range(3, block, 2):
        unit = block // units
        if block % units == 0 and unit <= 512 and unit % 64 == 0:
            return units
    return None


def gather_shards(
    n, ns, units,
    features, tissue, first_weight, first_gain, first_bias, second_weight, second_gain, second_bias,
):
    index = lax.axis_index("space")
    _, tiles_here, pixels, depth = features.shape
    block = tiles_here * pixels
    unit = block // units
    wide = first_weight.shape[1]
    width = second_weight.shape[1]
    total = n * block
    vmem = pl.BlockSpec(memory_space=pltpu.VMEM)
    anyspace = pl.BlockSpec(memory_space=pl.ANY)
    dma = pltpu.SemaphoreType.DMA
    second, stats1, stats2 = pl.pallas_call(
        functools.partial(gather_kernel, (n, ns, units, unit, tiles_here, pixels)),
        out_shape=(
            jax.ShapeDtypeStruct((width, total), jnp.float32),
            jax.ShapeDtypeStruct((8, wide), jnp.float32),
            jax.ShapeDtypeStruct((8, width), jnp.float32),
        ),
        in_specs=[pl.BlockSpec(memory_space=pltpu.SMEM), anyspace, vmem, vmem, vmem, vmem],
        out_specs=(anyspace, vmem, vmem),
        scratch_shapes=[
            pltpu.VMEM((total, depth), jnp.bfloat16),
            pltpu.VMEM((2, width, 2 * unit), jnp.float32),
            pltpu.VMEM((2, width, 128), jnp.float32),
            pltpu.VMEM((8, wide), jnp.float32),
            pltpu.VMEM((n, 8, wide), jnp.float32),
            pltpu.VMEM((ns, 8, wide), jnp.float32),
            pltpu.VMEM((ns, 8, width), jnp.float32),
            dma,
            dma((2,)),
            dma((units,)),
            dma((units,)),
            dma((4, units)),
            dma((units,)),
            dma((3, units)),
            dma((4, units)),
            dma((n,)),
            dma((n,)),
            dma((ns,)),
            dma((ns,)),
            dma((ns,)),
            dma((ns,)),
        ],
        compiler_params=pltpu.CompilerParams(
            collective_id=0, has_side_effects=True, vmem_limit_bytes=40 * 1024 * 1024
        ),
        cost_estimate=pl.CostEstimate(
            flops=2 * total * wide * (depth + width),
            bytes_accessed=4 * total * width + 2 * block * depth,
            transcendentals=0,
        ),
        name="gather_convs",
    )(
        tissue,
        features.reshape(block, depth),
        first_weight,
        first_gain[None, :],
        first_bias[None, :],
        second_weight,
    )
    gain_here = lax.dynamic_slice_in_dim(second_gain, index * width, width)[None, :]
    bias_here = lax.dynamic_slice_in_dim(second_bias, index * width, width)[None, :]
    lanes = total // 128
    steps = next(s for s in range(7, lanes + 1) if lanes % s == 0)
    cols = total // steps
    output = pl.pallas_call(
        finish_kernel,
        out_shape=jax.ShapeDtypeStruct((width, total), jnp.bfloat16),
        grid=(steps,),
        in_specs=[
            pl.BlockSpec((8, width), lambda i: (0, 0)),
            pl.BlockSpec((1, width), lambda i: (0, 0)),
            pl.BlockSpec((1, width), lambda i: (0, 0)),
            pl.BlockSpec((width, cols), lambda i: (0, i)),
        ],
        out_specs=pl.BlockSpec((width, cols), lambda i: (0, i)),
        compiler_params=pltpu.CompilerParams(vmem_limit_bytes=32 * 1024 * 1024),
        name="second_norm",
    )(stats2, gain_here, bias_here, second)
    return output[None], stats1[0], stats1[1], stats2[0], stats2[1]


def solution(mesh):
    n, ns = mesh.shape["space"], mesh.shape["section"]

    def shards(features, *rest):
        block = features.shape[1] * features.shape[2]
        units = units_of(block)
        width = rest[4].shape[1]
        if n == 8 and units is not None and width == 128:
            return gather_shards(n, ns, units, features, *rest)
        return plain_shards(features, *rest)

    in_specs = (
        P("section", "space", None, None),
        P("section", None),
        P(),
        P(),
        P(),
        P(None, "space"),
        P(),
        P(),
    )
    out_specs = (P("section", "space", None), P(), P(), P("space"), P("space"))
    return jax.shard_map(shards, mesh=mesh, in_specs=in_specs, out_specs=out_specs, check_vma=False)
```

```python
import functools

import jax
import jax.numpy as jnp
from jax import lax
from jax.experimental import pallas as pl
from jax.experimental.pallas import tpu as pltpu
from jax.sharding import PartitionSpec as P

EPS = 1e-05
MESH = pl.DeviceIdType.MESH
VMEM_ASKED = 32 * 1024 * 1024


def normalize(values, mean_val, var_val, gain, bias):
    return jnp.maximum(gain * (values - mean_val) * lax.rsqrt(var_val + EPS) + bias, 0.0)


def masked_sum(values, weight):
    return jnp.sum(values * weight, axis=(0, 1, 2))


def channel_first(values):
    batch, tiles_here, pixels, chans = values.shape
    return jnp.transpose(values, (0, 3, 1, 2)).reshape(batch, chans, tiles_here * pixels)


def plain_shards(
    features, tissue, first_weight, first_gain, first_bias, second_weight, second_gain, second_bias
):
    index = lax.axis_index("space")
    tiles_here = features.shape[1]
    pixels = features.shape[2]
    row_mask = tissue[0].astype(jnp.float32)
    own_mask = lax.dynamic_slice_in_dim(row_mask, index * tiles_here, tiles_here)
    own_weight = own_mask[None, :, None, None]
    local_count = jnp.sum(own_mask) * pixels
    first = jnp.einsum("mtpc,cd->mtpd", features, first_weight, preferred_element_type=jnp.float32)
    total, squares, count = lax.psum(
        (
            masked_sum(first, own_weight),
            jnp.sum(first * first * own_weight, axis=(0, 1, 2)),
            local_count,
        ),
        ("section", "space"),
    )
    first_mean = total / count
    first_var = squares / count - first_mean * first_mean
    activation = normalize(first, first_mean, first_var, first_gain, first_bias).astype(
        jnp.bfloat16
    )
    second = jnp.einsum(
        "mtpc,cd->mtpd",
        activation,
        lax.all_gather(second_weight, "space", axis=1, tiled=True),
        preferred_element_type=jnp.float32,
    )
    width_here = second_weight.shape[1]
    moved = lax.all_to_all(channel_first(second), "space", split_axis=1, concat_axis=2, tiled=True)
    row_weight = jnp.repeat(row_mask, pixels)[None, None, :]
    total_two, squares_two = lax.psum(
        (
            jnp.sum(moved * row_weight, axis=(0, 2)),
            jnp.sum(moved * moved * row_weight, axis=(0, 2)),
        ),
        "section",
    )
    second_mean = total_two / count
    second_var = squares_two / count - second_mean * second_mean
    gain_here = lax.dynamic_slice_in_dim(second_gain, index * width_here, width_here)
    bias_here = lax.dynamic_slice_in_dim(second_bias, index * width_here, width_here)
    output = normalize(
        moved, second_mean[:, None], second_var[:, None], gain_here[:, None], bias_here[:, None]
    ).astype(jnp.bfloat16)
    return (output, first_mean, first_var, second_mean, second_var)


def gather_kernel(
    shape,
    tissue_in,
    x_ref,
    w1_in,
    g1_in,
    b1_in,
    w2_in,
    g2_in,
    b2_in,
    second_ref,
    stats1_ref,
    stats2_ref,
    tissue,
    w1,
    g1,
    b1,
    w2,
    g2,
    b2,
    rows_all,
    acc,
    coef,
    st1,
    st2,
    st3,
    local_sem,
    send_a,
    send_b,
    send_p,
    send_f,
    recv_d,
    recv_p,
    st1_send,
    st1_recv,
    st2_send,
    st2_recv,
    st3_send,
    st3_recv,
):
    n, ns, units, unit, tiles_here, pixels = shape
    block = units * unit
    chunk = 2 * unit
    macros = (units + 1) // 2
    tiles_chip = 2 * tiles_here
    sec = lax.axis_index("section")
    me = lax.axis_index("space")
    core = lax.rem(me, 2)
    cx = lax.rem(me // 2, 2)
    cy = me // 4

    def chip_at(fx, fy):
        return lax.rem(cy + fy, 2) * 2 + lax.rem(cx + fx, 2)

    chip_b = chip_at(core, 1 - core)
    chip_a = chip_at(1 - core, core)
    chip_d = chip_at(1, 1)
    chip_o = chip_at(0, 0)
    dev_a = chip_a * 2 + core
    dev_b = chip_b * 2 + core
    partner = chip_o * 2 + (1 - core)

    def rows_of(chip, kind, k):
        start = (chip * 2 + kind) * block + lax.rem(k + kind, units) * unit
        return rows_all.at[pl.ds(pl.multiple_of(start, unit), unit)]

    def remote(src, dst, send, recv, device):
        return pltpu.make_async_remote_copy(
            src_ref=src, dst_ref=dst, send_sem=send, recv_sem=recv,
            device_id=(sec, device), device_id_type=MESH,
        )

    def own_src(k):
        start = lax.rem(k + core, units) * unit
        return x_ref.at[pl.ds(pl.multiple_of(start, unit), unit)]

    def own_copies(k):
        dst = rows_of(chip_o, core, k)
        return (
            remote(own_src(k), dst, send_a.at[k], recv_d.at[1, k], dev_a),
            remote(own_src(k), dst, send_b.at[k], recv_d.at[0, k], dev_b),
            remote(own_src(k), dst, send_p.at[0, k], recv_p.at[0, k], partner),
        )

    def start_own(k):
        for copy in own_copies(k):
            copy.start()

    def relay(group, chip, k):
        piece = rows_of(chip, core, k)
        return remote(piece, piece, send_p.at[group, k], recv_p.at[group, k], partner)

    def forward(k):
        piece = rows_of(chip_b, core, k)
        return remote(piece, piece, send_f.at[k], recv_d.at[2, k], dev_a)

    barrier = pltpu.get_barrier_semaphore()
    for step in range(1, n):
        pl.semaphore_signal(
            barrier, inc=1, device_id=(sec, lax.rem(me + step, n)), device_id_type=MESH
        )
    for step in range(1, ns):
        pl.semaphore_signal(
            barrier, inc=1, device_id=(lax.rem(sec + step, ns), me), device_id_type=MESH
        )
    own_rows = rows_all.at[pl.ds(pl.multiple_of(me * block, block), block)]
    pairs = (
        (tissue_in, tissue), (w1_in, w1), (x_ref, own_rows), (g1_in, g1), (b1_in, b1),
        (w2_in, w2), (g2_in, g2), (b2_in, b2),
    )
    fetches = [
        pltpu.make_async_copy(src, dst, local_sem.at[i]) for i, (src, dst) in enumerate(pairs)
    ]
    for fetch in fetches:
        fetch.start()
    pl.semaphore_wait(barrier, n - 1 + ns - 1)
    start_own(0)
    for fetch in fetches:
        fetch.wait()

    def tile_sums(t, carry):
        total, squares, count = carry
        weight = tissue[0, me * tiles_here + t].astype(jnp.float32)
        start = pl.multiple_of(me * block + t * pixels, 16)
        first = jnp.dot(
            rows_all[pl.ds(start, pixels), :], w1[...], preferred_element_type=jnp.float32
        )
        total += weight * jnp.sum(first, axis=0, keepdims=True)
        squares += weight * jnp.sum(first * first, axis=0, keepdims=True)
        return total, squares, count + weight * pixels

    wide = w1.shape[1]
    zero = jnp.zeros((1, wide), jnp.float32)
    total, squares, count = lax.fori_loop(0, tiles_here, tile_sums, (zero, zero, zero))
    mine = st1.at[me]
    mine[0:1, :] = total
    mine[1:2, :] = squares
    mine[2:3, :] = count
    mine[3:8, :] = jnp.zeros((5, wide), jnp.float32)

    def exchange(buf, slot, count_of, send, recv, device_of):
        copies = []
        for step in range(1, count_of):
            other = lax.rem(slot + step, count_of)
            copy = pltpu.make_async_remote_copy(
                src_ref=buf.at[slot], dst_ref=buf.at[slot],
                send_sem=send.at[step], recv_sem=recv.at[slot],
                device_id=device_of(other), device_id_type=MESH,
            )
            copy.start()
            copies.append((copy, other))
        return copies

    def collect(buf, copies, recv, send, device_of):
        for copy, other in copies:
            copy.wait_send()
        for step, (copy, other) in enumerate(copies):
            pltpu.make_async_remote_copy(
                src_ref=buf.at[other], dst_ref=buf.at[other],
                send_sem=send.at[step + 1], recv_sem=recv.at[other],
                device_id=device_of(other), device_id_type=MESH,
            ).wait_recv()

    def in_space(other):
        return (sec, other)

    def in_section(other):
        return (other, me)

    copies = exchange(st1, me, n, st1_send, st1_recv, in_space)
    lax.fori_loop(1, units, lambda k, c: (start_own(k), c)[1], 0)
    collect(st1, copies, st1_recv, st1_send, in_space)
    st2[sec] = jnp.sum(st1[...], axis=0)
    copies = exchange(st2, sec, ns, st2_send, st2_recv, in_section)
    collect(st2, copies, st2_recv, st2_send, in_section)
    sums = jnp.sum(st2[...], axis=0)
    count = sums[2:3, :]
    mean = sums[0:1, :] / count
    var = sums[1:2, :] / count - mean * mean
    scale = g1[...] * lax.rsqrt(var + EPS)
    stats1_ref[0:1, :] = mean
    stats1_ref[1:2, :] = var
    stats1_ref[2:8, :] = jnp.zeros((6, wide), jnp.float32)
    coef[0:1, :] = scale
    coef[1:2, :] = b1[...] - mean * scale
    coef[2:3, :] = count

    acc[...] = jnp.zeros_like(acc)

    def compute(chip, j):
        base = chip * (2 * block) + j * chunk
        rows = rows_all[pl.ds(pl.multiple_of(base, chunk), chunk), :]
        first = jnp.dot(rows, w1[...], preferred_element_type=jnp.float32)
        act = jnp.maximum(first * coef[0:1, :] + coef[1:2, :], 0.0).astype(jnp.bfloat16)
        second = jnp.dot(act, w2[...], preferred_element_type=jnp.float32).T
        lane = lax.broadcasted_iota(jnp.int32, (1, chunk), 1)
        tile = (j * chunk) // pixels
        mask = jnp.zeros((1, chunk), jnp.float32)
        for i in range(chunk // pixels + 2):
            at = tile + i
            held = tissue[0, chip * tiles_chip + lax.rem(at, tiles_chip)].astype(jnp.float32)
            low = at * pixels - j * chunk
            mask = jnp.where((lane >= low) & (lane < low + pixels), held, mask)
        kept = second * mask
        square = kept * second
        part = acc[0]
        part2 = acc[1]
        for i in range(chunk // 128):
            part += kept[:, i * 128:(i + 1) * 128]
            part2 += square[:, i * 128:(i + 1) * 128]
        acc[0] = part
        acc[1] = part2
        second_ref[:, pl.ds(pl.multiple_of(base, chunk), chunk)] = second

    def compute_macro(chip, m):
        compute(chip, m)

        @pl.when(m < macros - 1)
        def _():
            compute(chip, m + macros)

    def incoming(kind, chip, group, k):
        piece = rows_of(chip, kind, k)
        if group == "relay":
            return lambda g: remote(
                piece, piece, send_p.at[g, k], recv_p.at[g, k], partner
            ).wait_recv()
        return lambda g: remote(
            piece, piece, send_f.at[k], recv_d.at[g, k], dev_a
        ).wait_recv()

    def each_unit(m, fn):
        fn(2 * m)

        @pl.when(m < macros - 1)
        def _():
            fn(2 * m + 1)

    def own_step(m, c):
        each_unit(m, lambda k: incoming(1 - core, chip_o, "relay", k)(0))
        compute_macro(chip_o, m)
        return c

    def side_step(t, c):
        s = lax.rem(t, 2)
        m = t // 2
        chip = chip_at(lax.rem(core + s, 2), lax.rem(1 - core + s, 2))
        group = 1 + lax.rem(core + 1 + s, 2)

        def pass_b(k):
            incoming(core, chip_b, "direct", k)(0)
            forward(k).start()
            relay(2 - core, chip_b, k).start()

        def pass_a(k):
            incoming(core, chip_a, "direct", k)(1)
            relay(1 + core, chip_a, k).start()

        @pl.when(s == 0)
        def _():
            each_unit(m, pass_b)
            each_unit(m, pass_a)

        each_unit(m, lambda k: incoming(1 - core, chip, "relay", k)(group))
        compute_macro(chip, m)
        return c

    def last_step(m, c):
        def pass_on(k):
            incoming(core, chip_d, "direct", k)(2)
            relay(3, chip_d, k).start()

        each_unit(m, pass_on)
        each_unit(m, lambda k: incoming(1 - core, chip_d, "relay", k)(3))
        compute_macro(chip_d, m)
        return c

    lax.fori_loop(0, macros, own_step, 0)
    lax.fori_loop(0, 2 * macros, side_step, 0)
    lax.fori_loop(0, macros, last_step, 0)

    width = w2.shape[1]
    mine = st3.at[sec]
    mine[0:1, :] = jnp.sum(acc[0].T, axis=0, keepdims=True)
    mine[1:2, :] = jnp.sum(acc[1].T, axis=0, keepdims=True)
    mine[2:8, :] = jnp.zeros((6, width), jnp.float32)
    copies = exchange(st3, sec, ns, st3_send, st3_recv, in_section)

    def drain(k, c):
        for copy in own_copies(k):
            copy.wait_send()
        relay(1, chip_b, k).wait_send()
        relay(2, chip_a, k).wait_send()
        relay(3, chip_d, k).wait_send()
        forward(k).wait_send()
        return c

    lax.fori_loop(0, units, drain, 0)
    collect(st3, copies, st3_recv, st3_send, in_section)
    sums = jnp.sum(st3[...], axis=0)
    count = coef[2:3, 0:width]
    mean = sums[0:1, :] / count
    var = sums[1:2, :] / count - mean * mean
    scale = g2[pl.ds(me, 1), :] * lax.rsqrt(var + EPS)
    stats2_ref[0:1, :] = mean
    stats2_ref[1:2, :] = var
    stats2_ref[2:3, :] = scale
    stats2_ref[3:4, :] = b2[pl.ds(me, 1), :] - mean * scale
    stats2_ref[4:8, :] = jnp.zeros((4, width), jnp.float32)


def finish_kernel(cols, stats1, stats2, second, out, mean1, var1, mean2, var2):
    size = stats2.shape[1]
    scale = jnp.broadcast_to(stats2[2:3, :], (size, size)).T[:, 0:1]
    shift = jnp.broadcast_to(stats2[3:4, :], (size, size)).T[:, 0:1]
    start = pl.multiple_of(pl.program_id(0) * cols, cols)
    values = second[:, pl.ds(start, cols)]
    out[...] = jnp.maximum(values * scale + shift, 0.0).astype(out.dtype)
    mean1[...] = stats1[0:1, :]
    var1[...] = stats1[1:2, :]
    mean2[...] = stats2[0:1, :]
    var2[...] = stats2[1:2, :]


def units_of(block):
    for units in range(3, block, 2):
        unit = block // units
        if block % units == 0 and unit <= 512 and unit % 64 == 0:
            return units
    return None


def gather_shards(
    n, ns, units,
    features, tissue, first_weight, first_gain, first_bias, second_weight, second_gain, second_bias,
):
    _, tiles_here, pixels, depth = features.shape
    block = tiles_here * pixels
    unit = block // units
    wide = first_weight.shape[1]
    width = second_weight.shape[1]
    total = n * block
    vmem = pl.BlockSpec(memory_space=pltpu.VMEM)
    hbm = pl.BlockSpec(memory_space=pltpu.HBM)
    dma = pltpu.SemaphoreType.DMA
    second, stats1, stats2 = pl.pallas_call(
        functools.partial(gather_kernel, (n, ns, units, unit, tiles_here, pixels)),
        out_shape=(
            pltpu.VMEM((width, total), jnp.float32),
            pltpu.VMEM((8, wide), jnp.float32),
            pltpu.VMEM((8, width), jnp.float32),
        ),
        in_specs=[hbm] * 8,
        out_specs=(vmem, vmem, vmem),
        scratch_shapes=[
            pltpu.SMEM(tissue.shape, jnp.int32),
            pltpu.VMEM((depth, wide), jnp.bfloat16),
            pltpu.VMEM((1, wide), jnp.float32),
            pltpu.VMEM((1, wide), jnp.float32),
            pltpu.VMEM((wide, width), jnp.bfloat16),
            pltpu.VMEM((n, width), jnp.float32),
            pltpu.VMEM((n, width), jnp.float32),
            pltpu.VMEM((total, depth), jnp.bfloat16),
            pltpu.VMEM((2, width, 128), jnp.float32),
            pltpu.VMEM((8, wide), jnp.float32),
            pltpu.VMEM((n, 8, wide), jnp.float32),
            pltpu.VMEM((ns, 8, wide), jnp.float32),
            pltpu.VMEM((ns, 8, width), jnp.float32),
            dma((8,)),
            dma((units,)),
            dma((units,)),
            dma((4, units)),
            dma((units,)),
            dma((3, units)),
            dma((4, units)),
            dma((n,)),
            dma((n,)),
            dma((ns,)),
            dma((ns,)),
            dma((ns,)),
            dma((ns,)),
        ],
        compiler_params=pltpu.CompilerParams(
            collective_id=0, has_side_effects=True, vmem_limit_bytes=VMEM_ASKED
        ),
        cost_estimate=pl.CostEstimate(
            flops=2 * total * wide * (depth + width),
            bytes_accessed=2 * block * depth,
            transcendentals=0,
        ),
        name="gather_convs",
    )(
        *(
            pltpu.with_memory_space_constraint(array, pltpu.HBM)
            for array in (
                tissue,
                features.reshape(block, depth),
                first_weight,
                first_gain[None, :],
                first_bias[None, :],
                second_weight,
                second_gain.reshape(n, width),
                second_bias.reshape(n, width),
            )
        )
    )
    lanes = total // 128
    steps = next(s for s in range(7, lanes + 1) if lanes % s == 0)
    cols = total // steps
    output, mean1, var1, mean2, var2 = pl.pallas_call(
        functools.partial(finish_kernel, cols),
        out_shape=(
            jax.ShapeDtypeStruct((width, total), jnp.bfloat16),
            jax.ShapeDtypeStruct((1, wide), jnp.float32),
            jax.ShapeDtypeStruct((1, wide), jnp.float32),
            jax.ShapeDtypeStruct((1, width), jnp.float32),
            jax.ShapeDtypeStruct((1, width), jnp.float32),
        ),
        grid=(steps,),
        in_specs=[vmem, vmem, vmem],
        out_specs=(
            pl.BlockSpec((width, cols), lambda i: (0, i)),
            pl.BlockSpec((1, wide), lambda i: (0, 0)),
            pl.BlockSpec((1, wide), lambda i: (0, 0)),
            pl.BlockSpec((1, width), lambda i: (0, 0)),
            pl.BlockSpec((1, width), lambda i: (0, 0)),
        ),
        compiler_params=pltpu.CompilerParams(vmem_limit_bytes=VMEM_ASKED // 2),
        name="second_norm",
    )(*(pltpu.with_memory_space_constraint(x, pltpu.VMEM) for x in (stats1, stats2, second)))
    return output[None], mean1[0], var1[0], mean2[0], var2[0]


def solution(mesh):
    n, ns = mesh.shape["space"], mesh.shape["section"]

    def shards(features, *rest):
        block = features.shape[1] * features.shape[2]
        units = units_of(block)
        width = rest[4].shape[1]
        if n == 8 and units is not None and width == 128:
            return gather_shards(n, ns, units, features, *rest)
        return plain_shards(features, *rest)

    in_specs = (
        P("section", "space", None, None),
        P("section", None),
        P(),
        P(),
        P(),
        P(None, "space"),
        P(),
        P(),
    )
    out_specs = (P("section", "space", None), P(), P(), P("space"), P("space"))
    return jax.shard_map(shards, mesh=mesh, in_specs=in_specs, out_specs=out_specs, check_vma=False)
```

```python
import functools

import jax
import jax.numpy as jnp
from jax import lax
from jax.experimental import pallas as pl
from jax.experimental.pallas import tpu as pltpu
from jax.sharding import PartitionSpec as P

EPS = 1e-05
MESH = pl.DeviceIdType.MESH
VMEM_ASKED = 40 * 1024 * 1024


def normalize(values, mean_val, var_val, gain, bias):
    return jnp.maximum(gain * (values - mean_val) * lax.rsqrt(var_val + EPS) + bias, 0.0)


def masked_sum(values, weight):
    return jnp.sum(values * weight, axis=(0, 1, 2))


def channel_first(values):
    batch, tiles_here, pixels, chans = values.shape
    return jnp.transpose(values, (0, 3, 1, 2)).reshape(batch, chans, tiles_here * pixels)


def plain_shards(
    features, tissue, first_weight, first_gain, first_bias, second_weight, second_gain, second_bias
):
    index = lax.axis_index("space")
    tiles_here = features.shape[1]
    pixels = features.shape[2]
    row_mask = tissue[0].astype(jnp.float32)
    own_mask = lax.dynamic_slice_in_dim(row_mask, index * tiles_here, tiles_here)
    own_weight = own_mask[None, :, None, None]
    local_count = jnp.sum(own_mask) * pixels
    first = jnp.einsum("mtpc,cd->mtpd", features, first_weight, preferred_element_type=jnp.float32)
    total, squares, count = lax.psum(
        (
            masked_sum(first, own_weight),
            jnp.sum(first * first * own_weight, axis=(0, 1, 2)),
            local_count,
        ),
        ("section", "space"),
    )
    first_mean = total / count
    first_var = squares / count - first_mean * first_mean
    activation = normalize(first, first_mean, first_var, first_gain, first_bias).astype(
        jnp.bfloat16
    )
    second = jnp.einsum(
        "mtpc,cd->mtpd",
        activation,
        lax.all_gather(second_weight, "space", axis=1, tiled=True),
        preferred_element_type=jnp.float32,
    )
    width_here = second_weight.shape[1]
    moved = lax.all_to_all(channel_first(second), "space", split_axis=1, concat_axis=2, tiled=True)
    row_weight = jnp.repeat(row_mask, pixels)[None, None, :]
    total_two, squares_two = lax.psum(
        (
            jnp.sum(moved * row_weight, axis=(0, 2)),
            jnp.sum(moved * moved * row_weight, axis=(0, 2)),
        ),
        "section",
    )
    second_mean = total_two / count
    second_var = squares_two / count - second_mean * second_mean
    gain_here = lax.dynamic_slice_in_dim(second_gain, index * width_here, width_here)
    bias_here = lax.dynamic_slice_in_dim(second_bias, index * width_here, width_here)
    output = normalize(
        moved, second_mean[:, None], second_var[:, None], gain_here[:, None], bias_here[:, None]
    ).astype(jnp.bfloat16)
    return (output, first_mean, first_var, second_mean, second_var)


def gather_kernel(
    shape,
    tissue_in,
    x_ref,
    w1_in,
    g1_in,
    b1_in,
    w2_in,
    g2_in,
    b2_in,
    second_ref,
    stats1_ref,
    stats2_ref,
    tissue,
    w1,
    g1,
    b1,
    w2,
    g2,
    b2,
    rows_all,
    acts,
    acc,
    coef,
    st1,
    st2,
    st3,
    local_sem,
    send_a,
    send_b,
    send_p,
    send_f,
    recv_d,
    recv_p,
    st1_send,
    st1_recv,
    st2_send,
    st2_recv,
    st3_send,
    st3_recv,
):
    n, ns, units, unit, tiles_here, pixels = shape
    block = units * unit
    chunk = 2 * unit
    macros = (units + 1) // 2
    tiles_chip = 2 * tiles_here
    sec = lax.axis_index("section")
    me = lax.axis_index("space")
    core = lax.rem(me, 2)
    cx = lax.rem(me // 2, 2)
    cy = me // 4

    def chip_at(fx, fy):
        return lax.rem(cy + fy, 2) * 2 + lax.rem(cx + fx, 2)

    chip_b = chip_at(core, 1 - core)
    chip_a = chip_at(1 - core, core)
    chip_d = chip_at(1, 1)
    chip_o = chip_at(0, 0)
    dev_a = chip_a * 2 + core
    dev_b = chip_b * 2 + core
    partner = chip_o * 2 + (1 - core)

    def local_row(kind, k):
        return lax.rem(k + kind, units) * unit

    def rows_of(chip, k):
        start = chip * block + local_row(core, k)
        return rows_all.at[pl.ds(pl.multiple_of(start, unit), unit)]

    def acts_of(chip, kind, k):
        start = (chip * 2 + kind) * block + local_row(kind, k)
        return acts.at[pl.ds(pl.multiple_of(start, unit), unit)]

    def remote(src, dst, send, recv, device):
        return pltpu.make_async_remote_copy(
            src_ref=src, dst_ref=dst, send_sem=send, recv_sem=recv,
            device_id=(sec, device), device_id_type=MESH,
        )

    def own_copies(k):
        src = x_ref.at[pl.ds(pl.multiple_of(local_row(core, k), unit), unit)]
        dst = rows_of(chip_o, k)
        return (
            remote(src, dst, send_a.at[k], recv_d.at[1, k], dev_a),
            remote(src, dst, send_b.at[k], recv_d.at[0, k], dev_b),
        )

    def start_own(k):
        for copy in own_copies(k):
            copy.start()

    def relay(group, chip, kind, k):
        piece = acts_of(chip, kind, k)
        return remote(piece, piece, send_p.at[group, k], recv_p.at[group, k], partner)

    def forward(k):
        piece = rows_of(chip_b, k)
        return remote(piece, piece, send_f.at[k], recv_d.at[2, k], dev_a)

    def arrived(source, chip, k):
        piece = rows_of(chip, k)
        remote(piece, piece, send_f.at[k], recv_d.at[source, k], dev_a).wait_recv()

    barrier = pltpu.get_barrier_semaphore()
    for step in range(1, n):
        pl.semaphore_signal(
            barrier, inc=1, device_id=(sec, lax.rem(me + step, n)), device_id_type=MESH
        )
    for step in range(1, ns):
        pl.semaphore_signal(
            barrier, inc=1, device_id=(lax.rem(sec + step, ns), me), device_id_type=MESH
        )
    own_rows = rows_all.at[pl.ds(pl.multiple_of(chip_o * block, block), block)]
    pairs = (
        (tissue_in, tissue), (w1_in, w1), (x_ref, own_rows), (g1_in, g1), (b1_in, b1),
        (w2_in, w2), (g2_in, g2), (b2_in, b2),
    )
    fetches = [
        pltpu.make_async_copy(src, dst, local_sem.at[i]) for i, (src, dst) in enumerate(pairs)
    ]
    for fetch in fetches:
        fetch.start()
    pl.semaphore_wait(barrier, n - 1 + ns - 1)
    start_own(0)
    start_own(1)
    for fetch in fetches:
        fetch.wait()

    def tile_sums(t, carry):
        total, squares, count = carry
        weight = tissue[0, me * tiles_here + t].astype(jnp.float32)
        start = pl.multiple_of(chip_o * block + t * pixels, 16)
        first = jnp.dot(
            rows_all[pl.ds(start, pixels), :], w1[...], preferred_element_type=jnp.float32
        )
        total += weight * jnp.sum(first, axis=0, keepdims=True)
        squares += weight * jnp.sum(first * first, axis=0, keepdims=True)
        return total, squares, count + weight * pixels

    wide = w1.shape[1]
    zero = jnp.zeros((1, wide), jnp.float32)
    total, squares, count = lax.fori_loop(0, tiles_here, tile_sums, (zero, zero, zero))
    mine = st1.at[me]
    mine[0:1, :] = total
    mine[1:2, :] = squares
    mine[2:3, :] = count
    mine[3:8, :] = jnp.zeros((5, wide), jnp.float32)

    def exchange(buf, slot, count_of, send, recv, device_of):
        copies = []
        for step in range(1, count_of):
            other = lax.rem(slot + step, count_of)
            copy = pltpu.make_async_remote_copy(
                src_ref=buf.at[slot], dst_ref=buf.at[slot],
                send_sem=send.at[step], recv_sem=recv.at[slot],
                device_id=device_of(other), device_id_type=MESH,
            )
            copy.start()
            copies.append((copy, other))
        return copies

    def collect(buf, copies, recv, send, device_of):
        for copy, other in copies:
            copy.wait_send()
        for step, (copy, other) in enumerate(copies):
            pltpu.make_async_remote_copy(
                src_ref=buf.at[other], dst_ref=buf.at[other],
                send_sem=send.at[step + 1], recv_sem=recv.at[other],
                device_id=device_of(other), device_id_type=MESH,
            ).wait_recv()

    def in_space(other):
        return (sec, other)

    def in_section(other):
        return (other, me)

    copies = exchange(st1, me, n, st1_send, st1_recv, in_space)
    lax.fori_loop(2, units, lambda k, c: (start_own(k), c)[1], 0)
    collect(st1, copies, st1_recv, st1_send, in_space)
    st2[sec] = jnp.sum(st1[...], axis=0)
    copies = exchange(st2, sec, ns, st2_send, st2_recv, in_section)
    collect(st2, copies, st2_recv, st2_send, in_section)
    sums = jnp.sum(st2[...], axis=0)
    count = sums[2:3, :]
    mean = sums[0:1, :] / count
    var = sums[1:2, :] / count - mean * mean
    scale = g1[...] * lax.rsqrt(var + EPS)
    stats1_ref[0:1, :] = mean
    stats1_ref[1:2, :] = var
    stats1_ref[2:8, :] = jnp.zeros((6, wide), jnp.float32)
    coef[0:1, :] = scale
    coef[1:2, :] = b1[...] - mean * scale
    coef[2:3, :] = count

    acc[...] = jnp.zeros_like(acc)

    def activate(group, chip, k):
        rows = rows_of(chip, k)[...]
        first = jnp.dot(rows, w1[...], preferred_element_type=jnp.float32)
        act = jnp.maximum(first * coef[0:1, :] + coef[1:2, :], 0.0)
        acts_of(chip, core, k)[...] = act.astype(jnp.bfloat16)
        relay(group, chip, core, k).start()

    def compute(chip, j):
        base = chip * (2 * block) + j * chunk
        act = acts[pl.ds(pl.multiple_of(base, chunk), chunk), :]
        second = jnp.dot(act, w2[...], preferred_element_type=jnp.float32).T
        lane = lax.broadcasted_iota(jnp.int32, (1, chunk), 1)
        tile = (j * chunk) // pixels
        mask = jnp.zeros((1, chunk), jnp.float32)
        for i in range(chunk // pixels + 2):
            at = tile + i
            held = tissue[0, chip * tiles_chip + lax.rem(at, tiles_chip)].astype(jnp.float32)
            low = at * pixels - j * chunk
            mask = jnp.where((lane >= low) & (lane < low + pixels), held, mask)
        kept = second * mask
        square = kept * second
        part = acc[0]
        part2 = acc[1]
        for i in range(chunk // 128):
            part += kept[:, i * 128:(i + 1) * 128]
            part2 += square[:, i * 128:(i + 1) * 128]
        acc[0] = part
        acc[1] = part2
        second_ref[:, pl.ds(pl.multiple_of(base, chunk), chunk)] = second

    def each_unit(m, fn):
        fn(2 * m)

        @pl.when(m < macros - 1)
        def _():
            fn(2 * m + 1)

    def finish(group, chip, m):
        each_unit(m, lambda k: relay(group, chip, 1 - core, k).wait_recv())
        compute(chip, m)

        @pl.when(m < macros - 1)
        def _():
            compute(chip, m + macros)

    def side(s):
        chip = chip_at(lax.rem(core + s, 2), lax.rem(1 - core + s, 2))
        return 1 + lax.rem(core + 1 + s, 2), chip

    def finish_sides(m):
        def one(s, c):
            finish(*side(s), m)
            return c

        lax.fori_loop(0, 2, one, 0)

    last = macros - 1

    def own_step(m, c):
        each_unit(m, lambda k: activate(0, chip_o, k))

        @pl.when(m > 0)
        def _():
            finish(0, chip_o, m - 1)

        return c

    def side_step(m, c):
        def from_b(k):
            arrived(0, chip_b, k)
            forward(k).start()

        def from_a(k):
            arrived(1, chip_a, k)

        each_unit(m, from_b)
        each_unit(m, from_a)

        def one(s, c):
            group, chip = side(s)
            each_unit(m, lambda k: activate(group, chip, k))
            return c

        lax.fori_loop(0, 2, one, 0)

        @pl.when(m == 0)
        def _():
            finish(0, chip_o, last)

        @pl.when(m > 0)
        def _():
            finish_sides(m - 1)

        return c

    def last_step(m, c):
        def from_d(k):
            arrived(2, chip_d, k)
            activate(3, chip_d, k)

        @pl.when(m == 0)
        def _():
            finish_sides(last)

        each_unit(m, from_d)

        @pl.when(m > 0)
        def _():
            finish(3, chip_d, m - 1)

        return c

    lax.fori_loop(0, macros, own_step, 0)
    lax.fori_loop(0, macros, side_step, 0)
    lax.fori_loop(0, macros, last_step, 0)
    finish(3, chip_d, last)

    width = w2.shape[1]
    mine = st3.at[sec]
    mine[0:1, :] = jnp.sum(acc[0].T, axis=0, keepdims=True)
    mine[1:2, :] = jnp.sum(acc[1].T, axis=0, keepdims=True)
    mine[2:8, :] = jnp.zeros((6, width), jnp.float32)
    copies = exchange(st3, sec, ns, st3_send, st3_recv, in_section)

    def drain(k, c):
        for copy in own_copies(k):
            copy.wait_send()
        for group in range(4):
            relay(group, chip_o, core, k).wait_send()
        forward(k).wait_send()
        return c

    lax.fori_loop(0, units, drain, 0)
    collect(st3, copies, st3_recv, st3_send, in_section)
    sums = jnp.sum(st3[...], axis=0)
    count = coef[2:3, 0:width]
    mean = sums[0:1, :] / count
    var = sums[1:2, :] / count - mean * mean
    scale = g2[pl.ds(me, 1), :] * lax.rsqrt(var + EPS)
    stats2_ref[0:1, :] = mean
    stats2_ref[1:2, :] = var
    stats2_ref[2:3, :] = scale
    stats2_ref[3:4, :] = b2[pl.ds(me, 1), :] - mean * scale
    stats2_ref[4:8, :] = jnp.zeros((4, width), jnp.float32)


def finish_kernel(cols, stats1, stats2, second, out, mean1, var1, mean2, var2, held, sems):
    size = stats2.shape[1]
    scale = jnp.broadcast_to(stats2[2:3, :], (size, size)).T[:, 0:1]
    shift = jnp.broadcast_to(stats2[3:4, :], (size, size)).T[:, 0:1]

    def write(i):
        span = pl.ds(pl.multiple_of(i * cols, cols), cols)
        return pltpu.make_async_copy(held.at[:, span], out.at[:, span], sems.at[i])

    def one(i, c):
        span = pl.ds(pl.multiple_of(i * cols, cols), cols)
        values = second[:, span]
        held[:, span] = jnp.maximum(values * scale + shift, 0.0).astype(held.dtype)
        write(i).start()
        return c

    steps = sems.shape[0]
    lax.fori_loop(0, steps, one, 0)
    mean1[...] = stats1[0:1, :]
    var1[...] = stats1[1:2, :]
    mean2[...] = stats2[0:1, :]
    var2[...] = stats2[1:2, :]
    lax.fori_loop(0, steps, lambda i, c: (write(i).wait(), c)[1], 0)


def units_of(block):
    for units in range(3, block, 2):
        unit = block // units
        if block % units == 0 and unit <= 512 and unit % 64 == 0:
            return units
    return None


def gather_shards(
    n, ns, units,
    features, tissue, first_weight, first_gain, first_bias, second_weight, second_gain, second_bias,
):
    _, tiles_here, pixels, depth = features.shape
    block = tiles_here * pixels
    unit = block // units
    wide = first_weight.shape[1]
    width = second_weight.shape[1]
    total = n * block
    vmem = pl.BlockSpec(memory_space=pltpu.VMEM)
    hbm = pl.BlockSpec(memory_space=pltpu.HBM)
    dma = pltpu.SemaphoreType.DMA
    second, stats1, stats2 = pl.pallas_call(
        functools.partial(gather_kernel, (n, ns, units, unit, tiles_here, pixels)),
        out_shape=(
            pltpu.VMEM((width, total), jnp.float32),
            pltpu.VMEM((8, wide), jnp.float32),
            pltpu.VMEM((8, width), jnp.float32),
        ),
        in_specs=[hbm] * 8,
        out_specs=(vmem, vmem, vmem),
        scratch_shapes=[
            pltpu.SMEM(tissue.shape, jnp.int32),
            pltpu.VMEM((depth, wide), jnp.bfloat16),
            pltpu.VMEM((1, wide), jnp.float32),
            pltpu.VMEM((1, wide), jnp.float32),
            pltpu.VMEM((wide, width), jnp.bfloat16),
            pltpu.VMEM((n, width), jnp.float32),
            pltpu.VMEM((n, width), jnp.float32),
            pltpu.VMEM((total // 2, depth), jnp.bfloat16),
            pltpu.VMEM((total, wide), jnp.bfloat16),
            pltpu.VMEM((2, width, 128), jnp.float32),
            pltpu.VMEM((8, wide), jnp.float32),
            pltpu.VMEM((n, 8, wide), jnp.float32),
            pltpu.VMEM((ns, 8, wide), jnp.float32),
            pltpu.VMEM((ns, 8, width), jnp.float32),
            dma((8,)),
            dma((units,)),
            dma((units,)),
            dma((4, units)),
            dma((units,)),
            dma((3, units)),
            dma((4, units)),
            dma((n,)),
            dma((n,)),
            dma((ns,)),
            dma((ns,)),
            dma((ns,)),
            dma((ns,)),
        ],
        compiler_params=pltpu.CompilerParams(
            collective_id=0, has_side_effects=True, vmem_limit_bytes=VMEM_ASKED
        ),
        cost_estimate=pl.CostEstimate(
            flops=2 * total * wide * (depth + width),
            bytes_accessed=2 * block * depth,
            transcendentals=0,
        ),
        name="gather_convs",
    )(
        *(
            pltpu.with_memory_space_constraint(array, pltpu.HBM)
            for array in (
                tissue,
                features.reshape(block, depth),
                first_weight,
                first_gain[None, :],
                first_bias[None, :],
                second_weight,
                second_gain.reshape(n, width),
                second_bias.reshape(n, width),
            )
        )
    )
    lanes = total // 128
    steps = next(s for s in range(14, lanes + 1) if lanes % s == 0)
    cols = total // steps
    output, mean1, var1, mean2, var2 = pl.pallas_call(
        functools.partial(finish_kernel, cols),
        out_shape=(
            jax.ShapeDtypeStruct((width, total), jnp.bfloat16),
            jax.ShapeDtypeStruct((1, wide), jnp.float32),
            jax.ShapeDtypeStruct((1, wide), jnp.float32),
            jax.ShapeDtypeStruct((1, width), jnp.float32),
            jax.ShapeDtypeStruct((1, width), jnp.float32),
        ),
        in_specs=[vmem, vmem, vmem],
        out_specs=(hbm, vmem, vmem, vmem, vmem),
        scratch_shapes=[pltpu.VMEM((width, total), jnp.bfloat16), dma((steps,))],
        compiler_params=pltpu.CompilerParams(vmem_limit_bytes=VMEM_ASKED // 2),
        name="second_norm",
    )(*(pltpu.with_memory_space_constraint(x, pltpu.VMEM) for x in (stats1, stats2, second)))
    return output[None], mean1[0], var1[0], mean2[0], var2[0]


def solution(mesh):
    n, ns = mesh.shape["space"], mesh.shape["section"]

    def shards(features, *rest):
        block = features.shape[1] * features.shape[2]
        units = units_of(block)
        width = rest[4].shape[1]
        if n == 8 and units is not None and width == 128:
            return gather_shards(n, ns, units, features, *rest)
        return plain_shards(features, *rest)

    in_specs = (
        P("section", "space", None, None),
        P("section", None),
        P(),
        P(),
        P(),
        P(None, "space"),
        P(),
        P(),
    )
    out_specs = (P("section", "space", None), P(), P(), P("space"), P("space"))
    return jax.shard_map(shards, mesh=mesh, in_specs=in_specs, out_specs=out_specs, check_vma=False)
```

```python
import functools

import jax
import jax.numpy as jnp
from jax import lax
from jax.experimental import pallas as pl
from jax.experimental.pallas import tpu as pltpu
from jax.sharding import PartitionSpec as P

EPS = 1e-05
MESH = pl.DeviceIdType.MESH
VMEM_ASKED = 40 * 1024 * 1024


def normalize(values, mean_val, var_val, gain, bias):
    return jnp.maximum(gain * (values - mean_val) * lax.rsqrt(var_val + EPS) + bias, 0.0)


def masked_sum(values, weight):
    return jnp.sum(values * weight, axis=(0, 1, 2))


def channel_first(values):
    batch, tiles_here, pixels, chans = values.shape
    return jnp.transpose(values, (0, 3, 1, 2)).reshape(batch, chans, tiles_here * pixels)


def plain_shards(
    features, tissue, first_weight, first_gain, first_bias, second_weight, second_gain, second_bias
):
    index = lax.axis_index("space")
    tiles_here = features.shape[1]
    pixels = features.shape[2]
    row_mask = tissue[0].astype(jnp.float32)
    own_mask = lax.dynamic_slice_in_dim(row_mask, index * tiles_here, tiles_here)
    own_weight = own_mask[None, :, None, None]
    local_count = jnp.sum(own_mask) * pixels
    first = jnp.einsum("mtpc,cd->mtpd", features, first_weight, preferred_element_type=jnp.float32)
    total, squares, count = lax.psum(
        (
            masked_sum(first, own_weight),
            jnp.sum(first * first * own_weight, axis=(0, 1, 2)),
            local_count,
        ),
        ("section", "space"),
    )
    first_mean = total / count
    first_var = squares / count - first_mean * first_mean
    activation = normalize(first, first_mean, first_var, first_gain, first_bias).astype(
        jnp.bfloat16
    )
    second = jnp.einsum(
        "mtpc,cd->mtpd",
        activation,
        lax.all_gather(second_weight, "space", axis=1, tiled=True),
        preferred_element_type=jnp.float32,
    )
    width_here = second_weight.shape[1]
    moved = lax.all_to_all(channel_first(second), "space", split_axis=1, concat_axis=2, tiled=True)
    row_weight = jnp.repeat(row_mask, pixels)[None, None, :]
    total_two, squares_two = lax.psum(
        (
            jnp.sum(moved * row_weight, axis=(0, 2)),
            jnp.sum(moved * moved * row_weight, axis=(0, 2)),
        ),
        "section",
    )
    second_mean = total_two / count
    second_var = squares_two / count - second_mean * second_mean
    gain_here = lax.dynamic_slice_in_dim(second_gain, index * width_here, width_here)
    bias_here = lax.dynamic_slice_in_dim(second_bias, index * width_here, width_here)
    output = normalize(
        moved, second_mean[:, None], second_var[:, None], gain_here[:, None], bias_here[:, None]
    ).astype(jnp.bfloat16)
    return (output, first_mean, first_var, second_mean, second_var)


def gather_kernel(
    shape,
    tissue_in,
    x_ref,
    w1_in,
    g1_in,
    b1_in,
    w2_in,
    g2_in,
    b2_in,
    second_ref,
    stats1_ref,
    stats2_ref,
    tissue,
    w1,
    g1,
    b1,
    w2,
    g2,
    b2,
    rows_all,
    acts,
    acc,
    coef,
    st1,
    st2,
    st3,
    local_sem,
    send_a,
    send_b,
    send_p,
    send_f,
    recv_d,
    recv_p,
    st1_send,
    st1_recv,
    st2_send,
    st2_recv,
    st3_send,
    st3_recv,
):
    n, ns, units, unit, tiles_here, pixels = shape
    block = units * unit
    chunk = 2 * unit
    macros = (units + 1) // 2
    tiles_chip = 2 * tiles_here
    sec = lax.axis_index("section")
    me = lax.axis_index("space")
    core = lax.rem(me, 2)
    cx = lax.rem(me // 2, 2)
    cy = me // 4

    def chip_at(fx, fy):
        return lax.rem(cy + fy, 2) * 2 + lax.rem(cx + fx, 2)

    chip_b = chip_at(core, 1 - core)
    chip_a = chip_at(1 - core, core)
    chip_d = chip_at(1, 1)
    chip_o = chip_at(0, 0)
    dev_a = chip_a * 2 + core
    dev_b = chip_b * 2 + core
    partner = chip_o * 2 + (1 - core)

    def local_row(kind, k):
        return lax.rem(k + kind, units) * unit

    def rows_of(chip, k):
        start = chip * block + local_row(core, k)
        return rows_all.at[pl.ds(pl.multiple_of(start, unit), unit)]

    def acts_of(chip, kind, k):
        start = (chip * 2 + kind) * block + local_row(kind, k)
        return acts.at[pl.ds(pl.multiple_of(start, unit), unit)]

    def remote(src, dst, send, recv, device):
        return pltpu.make_async_remote_copy(
            src_ref=src, dst_ref=dst, send_sem=send, recv_sem=recv,
            device_id=(sec, device), device_id_type=MESH,
        )

    def own_copies(k):
        src = x_ref.at[pl.ds(pl.multiple_of(local_row(core, k), unit), unit)]
        dst = rows_of(chip_o, k)
        return (
            remote(src, dst, send_a.at[k], recv_d.at[1, k], dev_a),
            remote(src, dst, send_b.at[k], recv_d.at[0, k], dev_b),
        )

    def start_own(k):
        for copy in own_copies(k):
            copy.start()

    def relay(group, chip, kind, k):
        piece = acts_of(chip, kind, k)
        return remote(piece, piece, send_p.at[group, k], recv_p.at[group, k], partner)

    def forward(k):
        piece = rows_of(chip_b, k)
        return remote(piece, piece, send_f.at[k], recv_d.at[2, k], dev_a)

    def arrived(source, chip, k):
        piece = rows_of(chip, k)
        remote(piece, piece, send_f.at[k], recv_d.at[source, k], dev_a).wait_recv()

    barrier = pltpu.get_barrier_semaphore()
    for step in range(1, n):
        pl.semaphore_signal(
            barrier, inc=1, device_id=(sec, lax.rem(me + step, n)), device_id_type=MESH
        )
    for step in range(1, ns):
        pl.semaphore_signal(
            barrier, inc=1, device_id=(lax.rem(sec + step, ns), me), device_id_type=MESH
        )
    own_rows = rows_all.at[pl.ds(pl.multiple_of(chip_o * block, block), block)]
    pairs = (
        (tissue_in, tissue), (w1_in, w1), (x_ref, own_rows), (g1_in, g1), (b1_in, b1),
        (w2_in, w2), (g2_in, g2), (b2_in, b2),
    )
    fetches = [
        pltpu.make_async_copy(src, dst, local_sem.at[i]) for i, (src, dst) in enumerate(pairs)
    ]
    for fetch in fetches:
        fetch.start()
    pl.semaphore_wait(barrier, n - 1 + ns - 1)
    start_own(0)
    start_own(1)
    for fetch in fetches:
        fetch.wait()

    def tile_sums(t, carry):
        total, squares, count = carry
        weight = tissue[0, me * tiles_here + t].astype(jnp.float32)
        start = pl.multiple_of(chip_o * block + t * pixels, 16)
        first = jnp.dot(
            rows_all[pl.ds(start, pixels), :], w1[...], preferred_element_type=jnp.float32
        )
        total += weight * jnp.sum(first, axis=0, keepdims=True)
        squares += weight * jnp.sum(first * first, axis=0, keepdims=True)
        return total, squares, count + weight * pixels

    wide = w1.shape[1]
    zero = jnp.zeros((1, wide), jnp.float32)
    total, squares, count = lax.fori_loop(0, tiles_here, tile_sums, (zero, zero, zero))
    mine = st1.at[me]
    mine[0:1, :] = total
    mine[1:2, :] = squares
    mine[2:3, :] = count
    mine[3:8, :] = jnp.zeros((5, wide), jnp.float32)

    def exchange(buf, slot, count_of, send, recv, device_of):
        copies = []
        for step in range(1, count_of):
            other = lax.rem(slot + step, count_of)
            copy = pltpu.make_async_remote_copy(
                src_ref=buf.at[slot], dst_ref=buf.at[slot],
                send_sem=send.at[step], recv_sem=recv.at[slot],
                device_id=device_of(other), device_id_type=MESH,
            )
            copy.start()
            copies.append((copy, other))
        return copies

    def collect(buf, copies, recv, send, device_of):
        for copy, other in copies:
            copy.wait_send()
        for step, (copy, other) in enumerate(copies):
            pltpu.make_async_remote_copy(
                src_ref=buf.at[other], dst_ref=buf.at[other],
                send_sem=send.at[step + 1], recv_sem=recv.at[other],
                device_id=device_of(other), device_id_type=MESH,
            ).wait_recv()

    def in_space(other):
        return (sec, other)

    def in_section(other):
        return (other, me)

    copies = exchange(st1, me, n, st1_send, st1_recv, in_space)
    start_own(2)
    collect(st1, copies, st1_recv, st1_send, in_space)
    start_own(3)
    st2[sec] = jnp.sum(st1[...], axis=0)
    copies = exchange(st2, sec, ns, st2_send, st2_recv, in_section)
    collect(st2, copies, st2_recv, st2_send, in_section)
    sums = jnp.sum(st2[...], axis=0)
    count = sums[2:3, :]
    mean = sums[0:1, :] / count
    var = sums[1:2, :] / count - mean * mean
    scale = g1[...] * lax.rsqrt(var + EPS)
    stats1_ref[0:1, :] = mean
    stats1_ref[1:2, :] = var
    stats1_ref[2:8, :] = jnp.zeros((6, wide), jnp.float32)
    coef[0:1, :] = scale
    coef[1:2, :] = b1[...] - mean * scale
    coef[2:3, :] = count

    acc[...] = jnp.zeros_like(acc)

    def activate(group, chip, k):
        rows = rows_of(chip, k)[...]
        first = jnp.dot(rows, w1[...], preferred_element_type=jnp.float32)
        act = jnp.maximum(first * coef[0:1, :] + coef[1:2, :], 0.0)
        acts_of(chip, core, k)[...] = act.astype(jnp.bfloat16)
        relay(group, chip, core, k).start()

    def compute(chip, j):
        base = chip * (2 * block) + j * chunk
        act = acts[pl.ds(pl.multiple_of(base, chunk), chunk), :]
        second = jnp.dot(act, w2[...], preferred_element_type=jnp.float32).T
        lane = lax.broadcasted_iota(jnp.int32, (1, chunk), 1)
        tile = (j * chunk) // pixels
        mask = jnp.zeros((1, chunk), jnp.float32)
        for i in range(chunk // pixels + 2):
            at = tile + i
            held = tissue[0, chip * tiles_chip + lax.rem(at, tiles_chip)].astype(jnp.float32)
            low = at * pixels - j * chunk
            mask = jnp.where((lane >= low) & (lane < low + pixels), held, mask)
        kept = second * mask
        square = kept * second
        part = acc[0]
        part2 = acc[1]
        for i in range(chunk // 128):
            part += kept[:, i * 128:(i + 1) * 128]
            part2 += square[:, i * 128:(i + 1) * 128]
        acc[0] = part
        acc[1] = part2
        second_ref[:, pl.ds(pl.multiple_of(base, chunk), chunk)] = second

    def each_unit(m, fn):
        fn(2 * m)

        @pl.when(m < macros - 1)
        def _():
            fn(2 * m + 1)

    def finish(group, chip, m):
        each_unit(m, lambda k: relay(group, chip, 1 - core, k).wait_recv())
        compute(chip, m)

        @pl.when(m < macros - 1)
        def _():
            compute(chip, m + macros)

    def side(s):
        chip = chip_at(lax.rem(core + s, 2), lax.rem(1 - core + s, 2))
        return 1 + lax.rem(core + 1 + s, 2), chip

    def finish_sides(m):
        def one(s, c):
            finish(*side(s), m)
            return c

        lax.fori_loop(0, 2, one, 0)

    last = macros - 1
    ahead = 4

    def own_left(k):
        for copy in own_copies(k):
            copy.wait_send()

    def from_b(k):
        arrived(0, chip_b, k)
        forward(k).start()

    def own_step(m, c):
        @pl.when(m + ahead < units)
        def _():
            own_left(m)
            start_own(m + ahead)

        each_unit(m, lambda k: activate(0, chip_o, k))
        from_b(m)

        @pl.when(m > 0)
        def _():
            finish(0, chip_o, m - 1)

        return c

    def side_step(m, c):
        def from_a(k):
            arrived(1, chip_a, k)

        def later_b(k):
            pl.when(k >= macros)(lambda: from_b(k))

        each_unit(m, later_b)
        each_unit(m, from_a)

        def one(s, c):
            group, chip = side(s)
            each_unit(m, lambda k: activate(group, chip, k))
            return c

        lax.fori_loop(0, 2, one, 0)

        @pl.when(m == 0)
        def _():
            finish(0, chip_o, last)

        @pl.when(m > 0)
        def _():
            finish_sides(m - 1)

        return c

    def last_step(m, c):
        def from_d(k):
            arrived(2, chip_d, k)
            activate(3, chip_d, k)

        @pl.when(m == 0)
        def _():
            finish_sides(last)

        each_unit(m, from_d)

        @pl.when(m > 0)
        def _():
            finish(3, chip_d, m - 1)

        return c

    lax.fori_loop(0, macros, own_step, 0)

    def rest(k, c):
        own_left(k - ahead)
        start_own(k)
        return c

    lax.fori_loop(macros + ahead, units, rest, 0)
    lax.fori_loop(0, macros, side_step, 0)
    lax.fori_loop(0, macros, last_step, 0)
    finish(3, chip_d, last)

    width = w2.shape[1]
    mine = st3.at[sec]
    mine[0:1, :] = jnp.sum(acc[0].T, axis=0, keepdims=True)
    mine[1:2, :] = jnp.sum(acc[1].T, axis=0, keepdims=True)
    mine[2:8, :] = jnp.zeros((6, width), jnp.float32)
    copies = exchange(st3, sec, ns, st3_send, st3_recv, in_section)

    def drain(k, c):
        pl.when(k + ahead >= units)(lambda: own_left(k))
        for group in range(4):
            relay(group, chip_o, core, k).wait_send()
        forward(k).wait_send()
        return c

    lax.fori_loop(0, units, drain, 0)
    collect(st3, copies, st3_recv, st3_send, in_section)
    sums = jnp.sum(st3[...], axis=0)
    count = coef[2:3, 0:width]
    mean = sums[0:1, :] / count
    var = sums[1:2, :] / count - mean * mean
    scale = g2[pl.ds(me, 1), :] * lax.rsqrt(var + EPS)
    stats2_ref[0:1, :] = mean
    stats2_ref[1:2, :] = var
    stats2_ref[2:3, :] = scale
    stats2_ref[3:4, :] = b2[pl.ds(me, 1), :] - mean * scale
    stats2_ref[4:8, :] = jnp.zeros((4, width), jnp.float32)


def finish_kernel(cols, stats1, stats2, second, out, mean1, var1, mean2, var2, held, sems):
    size = stats2.shape[1]
    scale = jnp.broadcast_to(stats2[2:3, :], (size, size)).T[:, 0:1]
    shift = jnp.broadcast_to(stats2[3:4, :], (size, size)).T[:, 0:1]

    def write(i):
        span = pl.ds(pl.multiple_of(i * cols, cols), cols)
        return pltpu.make_async_copy(held.at[:, span], out.at[:, span], sems.at[i])

    def one(i, c):
        span = pl.ds(pl.multiple_of(i * cols, cols), cols)
        values = second[:, span]
        held[:, span] = jnp.maximum(values * scale + shift, 0.0).astype(held.dtype)
        write(i).start()
        return c

    steps = sems.shape[0]
    lax.fori_loop(0, steps, one, 0)
    mean1[...] = stats1[0:1, :]
    var1[...] = stats1[1:2, :]
    mean2[...] = stats2[0:1, :]
    var2[...] = stats2[1:2, :]
    lax.fori_loop(0, steps, lambda i, c: (write(i).wait(), c)[1], 0)


def units_of(block):
    for units in range(5, block, 2):
        unit = block // units
        if block % units == 0 and unit <= 512 and unit % 64 == 0:
            return units
    return None


def gather_shards(
    n, ns, units,
    features, tissue, first_weight, first_gain, first_bias, second_weight, second_gain, second_bias,
):
    _, tiles_here, pixels, depth = features.shape
    block = tiles_here * pixels
    unit = block // units
    wide = first_weight.shape[1]
    width = second_weight.shape[1]
    total = n * block
    vmem = pl.BlockSpec(memory_space=pltpu.VMEM)
    hbm = pl.BlockSpec(memory_space=pltpu.HBM)
    dma = pltpu.SemaphoreType.DMA
    second, stats1, stats2 = pl.pallas_call(
        functools.partial(gather_kernel, (n, ns, units, unit, tiles_here, pixels)),
        out_shape=(
            pltpu.VMEM((width, total), jnp.float32),
            pltpu.VMEM((8, wide), jnp.float32),
            pltpu.VMEM((8, width), jnp.float32),
        ),
        in_specs=[hbm] * 8,
        out_specs=(vmem, vmem, vmem),
        scratch_shapes=[
            pltpu.SMEM(tissue.shape, jnp.int32),
            pltpu.VMEM((depth, wide), jnp.bfloat16),
            pltpu.VMEM((1, wide), jnp.float32),
            pltpu.VMEM((1, wide), jnp.float32),
            pltpu.VMEM((wide, width), jnp.bfloat16),
            pltpu.VMEM((n, width), jnp.float32),
            pltpu.VMEM((n, width), jnp.float32),
            pltpu.VMEM((total // 2, depth), jnp.bfloat16),
            pltpu.VMEM((total, wide), jnp.bfloat16),
            pltpu.VMEM((2, width, 128), jnp.float32),
            pltpu.VMEM((8, wide), jnp.float32),
            pltpu.VMEM((n, 8, wide), jnp.float32),
            pltpu.VMEM((ns, 8, wide), jnp.float32),
            pltpu.VMEM((ns, 8, width), jnp.float32),
            dma((8,)),
            dma((units,)),
            dma((units,)),
            dma((4, units)),
            dma((units,)),
            dma((3, units)),
            dma((4, units)),
            dma((n,)),
            dma((n,)),
            dma((ns,)),
            dma((ns,)),
            dma((ns,)),
            dma((ns,)),
        ],
        compiler_params=pltpu.CompilerParams(
            collective_id=0, has_side_effects=True, vmem_limit_bytes=VMEM_ASKED
        ),
        cost_estimate=pl.CostEstimate(
            flops=2 * total * wide * (depth + width),
            bytes_accessed=2 * block * depth,
            transcendentals=0,
        ),
        name="gather_convs",
    )(
        *(
            pltpu.with_memory_space_constraint(array, pltpu.HBM)
            for array in (
                tissue,
                features.reshape(block, depth),
                first_weight,
                first_gain[None, :],
                first_bias[None, :],
                second_weight,
                second_gain.reshape(n, width),
                second_bias.reshape(n, width),
            )
        )
    )
    lanes = total // 128
    steps = next(s for s in range(14, lanes + 1) if lanes % s == 0)
    cols = total // steps
    output, mean1, var1, mean2, var2 = pl.pallas_call(
        functools.partial(finish_kernel, cols),
        out_shape=(
            jax.ShapeDtypeStruct((width, total), jnp.bfloat16),
            jax.ShapeDtypeStruct((1, wide), jnp.float32),
            jax.ShapeDtypeStruct((1, wide), jnp.float32),
            jax.ShapeDtypeStruct((1, width), jnp.float32),
            jax.ShapeDtypeStruct((1, width), jnp.float32),
        ),
        in_specs=[vmem, vmem, vmem],
        out_specs=(hbm, vmem, vmem, vmem, vmem),
        scratch_shapes=[pltpu.VMEM((width, total), jnp.bfloat16), dma((steps,))],
        compiler_params=pltpu.CompilerParams(vmem_limit_bytes=VMEM_ASKED // 2),
        name="second_norm",
    )(*(pltpu.with_memory_space_constraint(x, pltpu.VMEM) for x in (stats1, stats2, second)))
    return output[None], mean1[0], var1[0], mean2[0], var2[0]


def solution(mesh):
    n, ns = mesh.shape["space"], mesh.shape["section"]

    def shards(features, *rest):
        block = features.shape[1] * features.shape[2]
        units = units_of(block)
        width = rest[4].shape[1]
        if n == 8 and units is not None and width == 128:
            return gather_shards(n, ns, units, features, *rest)
        return plain_shards(features, *rest)

    in_specs = (
        P("section", "space", None, None),
        P("section", None),
        P(),
        P(),
        P(),
        P(None, "space"),
        P(),
        P(),
    )
    out_specs = (P("section", "space", None), P(), P(), P("space"), P("space"))
    return jax.shard_map(shards, mesh=mesh, in_specs=in_specs, out_specs=out_specs, check_vma=False)
```

```python
import functools

import jax
import jax.numpy as jnp
from jax import lax
from jax.experimental import pallas as pl
from jax.experimental.pallas import tpu as pltpu
from jax.sharding import PartitionSpec as P

EPS = 1e-05
MESH = pl.DeviceIdType.MESH
VMEM_ASKED = 40 * 1024 * 1024


def normalize(values, mean_val, var_val, gain, bias):
    return jnp.maximum(gain * (values - mean_val) * lax.rsqrt(var_val + EPS) + bias, 0.0)


def masked_sum(values, weight):
    return jnp.sum(values * weight, axis=(0, 1, 2))


def channel_first(values):
    batch, tiles_here, pixels, chans = values.shape
    return jnp.transpose(values, (0, 3, 1, 2)).reshape(batch, chans, tiles_here * pixels)


def plain_shards(
    features, tissue, first_weight, first_gain, first_bias, second_weight, second_gain, second_bias
):
    index = lax.axis_index("space")
    tiles_here = features.shape[1]
    pixels = features.shape[2]
    row_mask = tissue[0].astype(jnp.float32)
    own_mask = lax.dynamic_slice_in_dim(row_mask, index * tiles_here, tiles_here)
    own_weight = own_mask[None, :, None, None]
    local_count = jnp.sum(own_mask) * pixels
    first = jnp.einsum("mtpc,cd->mtpd", features, first_weight, preferred_element_type=jnp.float32)
    total, squares, count = lax.psum(
        (
            masked_sum(first, own_weight),
            jnp.sum(first * first * own_weight, axis=(0, 1, 2)),
            local_count,
        ),
        ("section", "space"),
    )
    first_mean = total / count
    first_var = squares / count - first_mean * first_mean
    activation = normalize(first, first_mean, first_var, first_gain, first_bias).astype(
        jnp.bfloat16
    )
    second = jnp.einsum(
        "mtpc,cd->mtpd",
        activation,
        lax.all_gather(second_weight, "space", axis=1, tiled=True),
        preferred_element_type=jnp.float32,
    )
    width_here = second_weight.shape[1]
    moved = lax.all_to_all(channel_first(second), "space", split_axis=1, concat_axis=2, tiled=True)
    row_weight = jnp.repeat(row_mask, pixels)[None, None, :]
    total_two, squares_two = lax.psum(
        (
            jnp.sum(moved * row_weight, axis=(0, 2)),
            jnp.sum(moved * moved * row_weight, axis=(0, 2)),
        ),
        "section",
    )
    second_mean = total_two / count
    second_var = squares_two / count - second_mean * second_mean
    gain_here = lax.dynamic_slice_in_dim(second_gain, index * width_here, width_here)
    bias_here = lax.dynamic_slice_in_dim(second_bias, index * width_here, width_here)
    output = normalize(
        moved, second_mean[:, None], second_var[:, None], gain_here[:, None], bias_here[:, None]
    ).astype(jnp.bfloat16)
    return (output, first_mean, first_var, second_mean, second_var)


def gather_kernel(
    shape,
    tissue_in,
    x_ref,
    w1_in,
    g1_in,
    b1_in,
    w2_in,
    g2_in,
    b2_in,
    second_ref,
    stats1_ref,
    stats2_ref,
    tissue,
    w1,
    g1,
    b1,
    w2,
    g2,
    b2,
    rows_all,
    acts,
    acc,
    coef,
    st1,
    st2,
    st3,
    local_sem,
    send_a,
    send_b,
    send_p,
    send_f,
    recv_d,
    recv_p,
    st1_send,
    st1_recv,
    st2_send,
    st2_recv,
    st3_send,
    st3_recv,
):
    n, ns, units, unit, tiles_here, pixels = shape
    block = units * unit
    chunk = 2 * unit
    macros = (units + 1) // 2
    tiles_chip = 2 * tiles_here
    sec = lax.axis_index("section")
    me = lax.axis_index("space")
    core = lax.rem(me, 2)
    cx = lax.rem(me // 2, 2)
    cy = me // 4

    def chip_at(fx, fy):
        return lax.rem(cy + fy, 2) * 2 + lax.rem(cx + fx, 2)

    chip_b = chip_at(core, 1 - core)
    chip_a = chip_at(1 - core, core)
    chip_d = chip_at(1, 1)
    chip_o = chip_at(0, 0)
    dev_a = chip_a * 2 + core
    dev_b = chip_b * 2 + core
    partner = chip_o * 2 + (1 - core)

    def local_row(kind, k):
        return lax.rem(k + kind, units) * unit

    def rows_of(chip, k):
        start = chip * block + local_row(core, k)
        return rows_all.at[pl.ds(pl.multiple_of(start, unit), unit)]

    def acts_of(chip, kind, k):
        start = (chip * 2 + kind) * block + local_row(kind, k)
        return acts.at[pl.ds(pl.multiple_of(start, unit), unit)]

    def remote(src, dst, send, recv, device):
        return pltpu.make_async_remote_copy(
            src_ref=src, dst_ref=dst, send_sem=send, recv_sem=recv,
            device_id=(sec, device), device_id_type=MESH,
        )

    def own_copies(k):
        src = x_ref.at[pl.ds(pl.multiple_of(local_row(core, k), unit), unit)]
        dst = rows_of(chip_o, k)
        return (
            remote(src, dst, send_a.at[k], recv_d.at[1, k], dev_a),
            remote(src, dst, send_b.at[k], recv_d.at[0, k], dev_b),
        )

    def start_own(k):
        for copy in own_copies(k):
            copy.start()

    def relay(group, chip, kind, k):
        piece = acts_of(chip, kind, k)
        return remote(piece, piece, send_p.at[group, k], recv_p.at[group, k], partner)

    def forward(k):
        piece = rows_of(chip_b, k)
        return remote(piece, piece, send_f.at[k], recv_d.at[2, k], dev_a)

    def arrived(source, chip, k):
        piece = rows_of(chip, k)
        remote(piece, piece, send_f.at[k], recv_d.at[source, k], dev_a).wait_recv()

    barrier = pltpu.get_barrier_semaphore()
    for step in range(1, n):
        pl.semaphore_signal(
            barrier, inc=1, device_id=(sec, lax.rem(me + step, n)), device_id_type=MESH
        )
    for step in range(1, ns):
        pl.semaphore_signal(
            barrier, inc=1, device_id=(lax.rem(sec + step, ns), me), device_id_type=MESH
        )
    own_rows = rows_all.at[pl.ds(pl.multiple_of(chip_o * block, block), block)]
    pairs = (
        (tissue_in, tissue), (w1_in, w1), (x_ref, own_rows), (g1_in, g1), (b1_in, b1),
        (w2_in, w2), (g2_in, g2), (b2_in, b2),
    )
    fetches = [
        pltpu.make_async_copy(src, dst, local_sem.at[i]) for i, (src, dst) in enumerate(pairs)
    ]
    for fetch in fetches:
        fetch.start()
    pl.semaphore_wait(barrier, n - 1 + ns - 1)
    start_own(0)
    start_own(1)
    for fetch in fetches:
        fetch.wait()

    def tile_sums(t, carry):
        total, squares, count = carry
        weight = tissue[0, me * tiles_here + t].astype(jnp.float32)
        start = pl.multiple_of(chip_o * block + t * pixels, 16)
        first = jnp.dot(
            rows_all[pl.ds(start, pixels), :], w1[...], preferred_element_type=jnp.float32
        )
        total += weight * jnp.sum(first, axis=0, keepdims=True)
        squares += weight * jnp.sum(first * first, axis=0, keepdims=True)
        return total, squares, count + weight * pixels

    wide = w1.shape[1]
    zero = jnp.zeros((1, wide), jnp.float32)
    total, squares, count = lax.fori_loop(0, tiles_here, tile_sums, (zero, zero, zero))
    mine = st1.at[me]
    mine[0:1, :] = total
    mine[1:2, :] = squares
    mine[2:3, :] = count
    mine[3:8, :] = jnp.zeros((5, wide), jnp.float32)

    def exchange(buf, slot, count_of, send, recv, device_of):
        copies = []
        for step in range(1, count_of):
            other = lax.rem(slot + step, count_of)
            copy = pltpu.make_async_remote_copy(
                src_ref=buf.at[slot], dst_ref=buf.at[slot],
                send_sem=send.at[step], recv_sem=recv.at[slot],
                device_id=device_of(other), device_id_type=MESH,
            )
            copy.start()
            copies.append((copy, other))
        return copies

    def collect(buf, copies, recv, send, device_of):
        for copy, other in copies:
            copy.wait_send()
        for step, (copy, other) in enumerate(copies):
            pltpu.make_async_remote_copy(
                src_ref=buf.at[other], dst_ref=buf.at[other],
                send_sem=send.at[step + 1], recv_sem=recv.at[other],
                device_id=device_of(other), device_id_type=MESH,
            ).wait_recv()

    def in_space(other):
        return (sec, other)

    def in_section(other):
        return (other, me)

    copies = exchange(st1, me, n, st1_send, st1_recv, in_space)
    lax.fori_loop(2, units, lambda k, c: (start_own(k), c)[1], 0)
    collect(st1, copies, st1_recv, st1_send, in_space)
    st2[sec] = jnp.sum(st1[...], axis=0)
    copies = exchange(st2, sec, ns, st2_send, st2_recv, in_section)
    collect(st2, copies, st2_recv, st2_send, in_section)
    sums = jnp.sum(st2[...], axis=0)
    count = sums[2:3, :]
    mean = sums[0:1, :] / count
    var = sums[1:2, :] / count - mean * mean
    scale = g1[...] * lax.rsqrt(var + EPS)
    stats1_ref[0:1, :] = mean
    stats1_ref[1:2, :] = var
    stats1_ref[2:8, :] = jnp.zeros((6, wide), jnp.float32)
    coef[0:1, :] = scale
    coef[1:2, :] = b1[...] - mean * scale
    coef[2:3, :] = count

    acc[...] = jnp.zeros_like(acc)

    def activate(group, chip, k):
        rows = rows_of(chip, k)[...]
        first = jnp.dot(rows, w1[...], preferred_element_type=jnp.float32)
        act = jnp.maximum(first * coef[0:1, :] + coef[1:2, :], 0.0)
        acts_of(chip, core, k)[...] = act.astype(jnp.bfloat16)
        relay(group, chip, core, k).start()

    def compute(chip, j):
        base = chip * (2 * block) + j * chunk
        act = acts[pl.ds(pl.multiple_of(base, chunk), chunk), :]
        second = jnp.dot(act, w2[...], preferred_element_type=jnp.float32).T
        lane = lax.broadcasted_iota(jnp.int32, (1, chunk), 1)
        tile = (j * chunk) // pixels
        mask = jnp.zeros((1, chunk), jnp.float32)
        for i in range(chunk // pixels + 2):
            at = tile + i
            held = tissue[0, chip * tiles_chip + lax.rem(at, tiles_chip)].astype(jnp.float32)
            low = at * pixels - j * chunk
            mask = jnp.where((lane >= low) & (lane < low + pixels), held, mask)
        kept = second * mask
        square = kept * second
        part = acc[0]
        part2 = acc[1]
        for i in range(chunk // 128):
            part += kept[:, i * 128:(i + 1) * 128]
            part2 += square[:, i * 128:(i + 1) * 128]
        acc[0] = part
        acc[1] = part2
        second_ref[:, pl.ds(pl.multiple_of(base, chunk), chunk)] = second

    def each_unit(m, fn):
        fn(2 * m)

        @pl.when(m < macros - 1)
        def _():
            fn(2 * m + 1)

    def finish(group, chip, m):
        each_unit(m, lambda k: relay(group, chip, 1 - core, k).wait_recv())
        compute(chip, m)

        @pl.when(m < macros - 1)
        def _():
            compute(chip, m + macros)

    def side(s):
        chip = chip_at(lax.rem(core + s, 2), lax.rem(1 - core + s, 2))
        return 1 + lax.rem(core + 1 + s, 2), chip

    def finish_sides(m):
        def one(s, c):
            finish(*side(s), m)
            return c

        lax.fori_loop(0, 2, one, 0)

    last = macros - 1

    def own_step(m, c):
        each_unit(m, lambda k: activate(0, chip_o, k))

        @pl.when(m > 0)
        def _():
            finish(0, chip_o, m - 1)

        return c

    def side_step(m, c):
        def from_b(k):
            arrived(0, chip_b, k)
            forward(k).start()

        def from_a(k):
            arrived(1, chip_a, k)

        each_unit(m, from_b)
        each_unit(m, from_a)

        def one(s, c):
            group, chip = side(s)
            each_unit(m, lambda k: activate(group, chip, k))
            return c

        lax.fori_loop(0, 2, one, 0)

        @pl.when(m == 0)
        def _():
            finish(0, chip_o, last)

        @pl.when(m > 0)
        def _():
            finish_sides(m - 1)

        return c

    def last_step(m, c):
        def from_d(k):
            arrived(2, chip_d, k)
            activate(3, chip_d, k)

        @pl.when(m == 0)
        def _():
            finish_sides(last)

        each_unit(m, from_d)

        @pl.when(m > 0)
        def _():
            finish(3, chip_d, m - 1)

        return c

    lax.fori_loop(0, macros, own_step, 0)
    lax.fori_loop(0, macros, side_step, 0)
    lax.fori_loop(0, macros, last_step, 0)
    finish(3, chip_d, last)

    width = w2.shape[1]
    mine = st3.at[sec]
    mine[0:1, :] = jnp.sum(acc[0].T, axis=0, keepdims=True)
    mine[1:2, :] = jnp.sum(acc[1].T, axis=0, keepdims=True)
    mine[2:8, :] = jnp.zeros((6, width), jnp.float32)
    copies = exchange(st3, sec, ns, st3_send, st3_recv, in_section)

    def drain(k, c):
        for copy in own_copies(k):
            copy.wait_send()
        for group in range(4):
            relay(group, chip_o, core, k).wait_send()
        forward(k).wait_send()
        return c

    lax.fori_loop(0, units, drain, 0)
    collect(st3, copies, st3_recv, st3_send, in_section)
    sums = jnp.sum(st3[...], axis=0)
    count = coef[2:3, 0:width]
    mean = sums[0:1, :] / count
    var = sums[1:2, :] / count - mean * mean
    scale = g2[pl.ds(me, 1), :] * lax.rsqrt(var + EPS)
    stats2_ref[0:1, :] = mean
    stats2_ref[1:2, :] = var
    stats2_ref[2:3, :] = scale
    stats2_ref[3:4, :] = b2[pl.ds(me, 1), :] - mean * scale
    stats2_ref[4:8, :] = jnp.zeros((4, width), jnp.float32)


def finish_kernel(
    cols, stats1, stats2, second, out, mean1, var1, mean2, var2,
    held, rows1, rows2, sems, stat_sems,
):
    size = stats2.shape[1]
    scale = jnp.broadcast_to(stats2[2:3, :], (size, size)).T
    shift = jnp.broadcast_to(stats2[3:4, :], (size, size)).T
    for i in range(2):
        rows1[i] = stats1[i:i + 1, :]
        rows2[i] = stats2[i:i + 1, :]
    small = [
        pltpu.make_async_copy(src, dst, stat_sems.at[i])
        for i, (src, dst) in enumerate(
            ((rows1.at[0], mean1), (rows1.at[1], var1), (rows2.at[0], mean2), (rows2.at[1], var2))
        )
    ]
    for copy in small:
        copy.start()

    def write(i):
        span = pl.ds(pl.multiple_of(i * cols, cols), cols)
        return pltpu.make_async_copy(held.at[:, span], out.at[:, span], sems.at[i])

    def one(i, c):
        for j in range(cols // size):
            span = pl.ds(pl.multiple_of(i * cols + j * size, size), size)
            values = second[:, span] * scale + shift
            held[:, span] = jnp.maximum(values, 0.0).astype(held.dtype)
        write(i).start()
        return c

    steps = sems.shape[0]
    lax.fori_loop(0, steps, one, 0)
    for copy in small:
        copy.wait()
    lax.fori_loop(0, steps, lambda i, c: (write(i).wait(), c)[1], 0)


def units_of(block):
    for units in range(3, block, 2):
        unit = block // units
        if block % units == 0 and unit <= 512 and unit % 64 == 0:
            return units
    return None


def gather_shards(
    n, ns, units,
    features, tissue, first_weight, first_gain, first_bias, second_weight, second_gain, second_bias,
):
    _, tiles_here, pixels, depth = features.shape
    block = tiles_here * pixels
    unit = block // units
    wide = first_weight.shape[1]
    width = second_weight.shape[1]
    total = n * block
    vmem = pl.BlockSpec(memory_space=pltpu.VMEM)
    hbm = pl.BlockSpec(memory_space=pltpu.HBM)
    dma = pltpu.SemaphoreType.DMA
    second, stats1, stats2 = pl.pallas_call(
        functools.partial(gather_kernel, (n, ns, units, unit, tiles_here, pixels)),
        out_shape=(
            pltpu.VMEM((width, total), jnp.float32),
            pltpu.VMEM((8, wide), jnp.float32),
            pltpu.VMEM((8, width), jnp.float32),
        ),
        in_specs=[hbm] * 8,
        out_specs=(vmem, vmem, vmem),
        scratch_shapes=[
            pltpu.SMEM(tissue.shape, jnp.int32),
            pltpu.VMEM((depth, wide), jnp.bfloat16),
            pltpu.VMEM((1, wide), jnp.float32),
            pltpu.VMEM((1, wide), jnp.float32),
            pltpu.VMEM((wide, width), jnp.bfloat16),
            pltpu.VMEM((n, width), jnp.float32),
            pltpu.VMEM((n, width), jnp.float32),
            pltpu.VMEM((total // 2, depth), jnp.bfloat16),
            pltpu.VMEM((total, wide), jnp.bfloat16),
            pltpu.VMEM((2, width, 128), jnp.float32),
            pltpu.VMEM((8, wide), jnp.float32),
            pltpu.VMEM((n, 8, wide), jnp.float32),
            pltpu.VMEM((ns, 8, wide), jnp.float32),
            pltpu.VMEM((ns, 8, width), jnp.float32),
            dma((8,)),
            dma((units,)),
            dma((units,)),
            dma((4, units)),
            dma((units,)),
            dma((3, units)),
            dma((4, units)),
            dma((n,)),
            dma((n,)),
            dma((ns,)),
            dma((ns,)),
            dma((ns,)),
            dma((ns,)),
        ],
        compiler_params=pltpu.CompilerParams(
            collective_id=0, has_side_effects=True, vmem_limit_bytes=VMEM_ASKED
        ),
        cost_estimate=pl.CostEstimate(
            flops=2 * total * wide * (depth + width),
            bytes_accessed=2 * block * depth,
            transcendentals=0,
        ),
        name="gather_convs",
    )(
        *(
            pltpu.with_memory_space_constraint(array, pltpu.HBM)
            for array in (
                tissue,
                features.reshape(block, depth),
                first_weight,
                first_gain[None, :],
                first_bias[None, :],
                second_weight,
                second_gain.reshape(n, width),
                second_bias.reshape(n, width),
            )
        )
    )
    lanes = total // 128
    steps = next(s for s in range(14, lanes + 1) if lanes % s == 0)
    cols = total // steps
    output, mean1, var1, mean2, var2 = pl.pallas_call(
        functools.partial(finish_kernel, cols),
        out_shape=(
            jax.ShapeDtypeStruct((width, total), jnp.bfloat16),
            jax.ShapeDtypeStruct((1, wide), jnp.float32),
            jax.ShapeDtypeStruct((1, wide), jnp.float32),
            jax.ShapeDtypeStruct((1, width), jnp.float32),
            jax.ShapeDtypeStruct((1, width), jnp.float32),
        ),
        in_specs=[vmem, vmem, vmem],
        out_specs=(hbm,) * 5,
        scratch_shapes=[
            pltpu.VMEM((width, total), jnp.bfloat16),
            pltpu.VMEM((2, 1, wide), jnp.float32),
            pltpu.VMEM((2, 1, width), jnp.float32),
            dma((steps,)),
            dma((4,)),
        ],
        compiler_params=pltpu.CompilerParams(vmem_limit_bytes=VMEM_ASKED // 2),
        name="second_norm",
    )(*(pltpu.with_memory_space_constraint(x, pltpu.VMEM) for x in (stats1, stats2, second)))
    return output[None], mean1[0], var1[0], mean2[0], var2[0]


def solution(mesh):
    n, ns = mesh.shape["space"], mesh.shape["section"]

    def shards(features, *rest):
        block = features.shape[1] * features.shape[2]
        units = units_of(block)
        width = rest[4].shape[1]
        if n == 8 and units is not None and width == 128:
            return gather_shards(n, ns, units, features, *rest)
        return plain_shards(features, *rest)

    in_specs = (
        P("section", "space", None, None),
        P("section", None),
        P(),
        P(),
        P(),
        P(None, "space"),
        P(),
        P(),
    )
    out_specs = (P("section", "space", None), P(), P(), P("space"), P("space"))
    return jax.shard_map(shards, mesh=mesh, in_specs=in_specs, out_specs=out_specs, check_vma=False)
```

```python
import functools

import jax
import jax.numpy as jnp
from jax import lax
from jax.experimental import pallas as pl
from jax.experimental.pallas import tpu as pltpu
from jax.sharding import PartitionSpec as P

EPS = 1e-05
MESH = pl.DeviceIdType.MESH
VMEM_ASKED = 40 * 1024 * 1024


def normalize(values, mean_val, var_val, gain, bias):
    return jnp.maximum(gain * (values - mean_val) * lax.rsqrt(var_val + EPS) + bias, 0.0)


def masked_sum(values, weight):
    return jnp.sum(values * weight, axis=(0, 1, 2))


def channel_first(values):
    batch, tiles_here, pixels, chans = values.shape
    return jnp.transpose(values, (0, 3, 1, 2)).reshape(batch, chans, tiles_here * pixels)


def plain_shards(
    features, tissue, first_weight, first_gain, first_bias, second_weight, second_gain, second_bias
):
    index = lax.axis_index("space")
    tiles_here = features.shape[1]
    pixels = features.shape[2]
    row_mask = tissue[0].astype(jnp.float32)
    own_mask = lax.dynamic_slice_in_dim(row_mask, index * tiles_here, tiles_here)
    own_weight = own_mask[None, :, None, None]
    local_count = jnp.sum(own_mask) * pixels
    first = jnp.einsum("mtpc,cd->mtpd", features, first_weight, preferred_element_type=jnp.float32)
    total, squares, count = lax.psum(
        (
            masked_sum(first, own_weight),
            jnp.sum(first * first * own_weight, axis=(0, 1, 2)),
            local_count,
        ),
        ("section", "space"),
    )
    first_mean = total / count
    first_var = squares / count - first_mean * first_mean
    activation = normalize(first, first_mean, first_var, first_gain, first_bias).astype(
        jnp.bfloat16
    )
    second = jnp.einsum(
        "mtpc,cd->mtpd",
        activation,
        lax.all_gather(second_weight, "space", axis=1, tiled=True),
        preferred_element_type=jnp.float32,
    )
    width_here = second_weight.shape[1]
    moved = lax.all_to_all(channel_first(second), "space", split_axis=1, concat_axis=2, tiled=True)
    row_weight = jnp.repeat(row_mask, pixels)[None, None, :]
    total_two, squares_two = lax.psum(
        (
            jnp.sum(moved * row_weight, axis=(0, 2)),
            jnp.sum(moved * moved * row_weight, axis=(0, 2)),
        ),
        "section",
    )
    second_mean = total_two / count
    second_var = squares_two / count - second_mean * second_mean
    gain_here = lax.dynamic_slice_in_dim(second_gain, index * width_here, width_here)
    bias_here = lax.dynamic_slice_in_dim(second_bias, index * width_here, width_here)
    output = normalize(
        moved, second_mean[:, None], second_var[:, None], gain_here[:, None], bias_here[:, None]
    ).astype(jnp.bfloat16)
    return (output, first_mean, first_var, second_mean, second_var)


def gather_kernel(
    shape,
    tissue_in,
    x_ref,
    w1_in,
    g1_in,
    b1_in,
    w2_in,
    g2_in,
    b2_in,
    second_ref,
    stats1_ref,
    stats2_ref,
    tissue,
    w1,
    g1,
    b1,
    w2,
    g2,
    b2,
    rows_all,
    acts,
    acc,
    coef,
    st1,
    st2,
    st3,
    local_sem,
    send_a,
    send_b,
    send_p,
    send_f,
    recv_d,
    recv_p,
    st1_send,
    st1_recv,
    st2_send,
    st2_recv,
    st3_send,
    st3_recv,
):
    n, ns, units, unit, tiles_here, pixels = shape
    block = units * unit
    chunk = 2 * unit
    macros = (units + 1) // 2
    tiles_chip = 2 * tiles_here
    sec = lax.axis_index("section")
    me = lax.axis_index("space")
    core = lax.rem(me, 2)
    cx = lax.rem(me // 2, 2)
    cy = me // 4

    def chip_at(fx, fy):
        return lax.rem(cy + fy, 2) * 2 + lax.rem(cx + fx, 2)

    chip_b = chip_at(core, 1 - core)
    chip_a = chip_at(1 - core, core)
    chip_d = chip_at(1, 1)
    chip_o = chip_at(0, 0)
    dev_a = chip_a * 2 + core
    dev_b = chip_b * 2 + core
    partner = chip_o * 2 + (1 - core)

    def local_row(kind, k):
        return lax.rem(k + kind, units) * unit

    def rows_of(chip, k):
        start = chip * block + local_row(core, k)
        return rows_all.at[pl.ds(pl.multiple_of(start, unit), unit)]

    def acts_of(chip, kind, k):
        start = (chip * 2 + kind) * block + local_row(kind, k)
        return acts.at[pl.ds(pl.multiple_of(start, unit), unit)]

    def remote(src, dst, send, recv, device):
        return pltpu.make_async_remote_copy(
            src_ref=src, dst_ref=dst, send_sem=send, recv_sem=recv,
            device_id=(sec, device), device_id_type=MESH,
        )

    def own_copies(k):
        src = x_ref.at[pl.ds(pl.multiple_of(local_row(core, k), unit), unit)]
        dst = rows_of(chip_o, k)
        return (
            remote(src, dst, send_a.at[k], recv_d.at[1, k], dev_a),
            remote(src, dst, send_b.at[k], recv_d.at[0, k], dev_b),
        )

    def start_own(k):
        for copy in own_copies(k):
            copy.start()

    def relay(group, chip, kind, k):
        piece = acts_of(chip, kind, k)
        return remote(piece, piece, send_p.at[group, k], recv_p.at[group, k], partner)

    def forward(k):
        piece = rows_of(chip_b, k)
        return remote(piece, piece, send_f.at[k], recv_d.at[2, k], dev_a)

    def arrived(source, chip, k):
        piece = rows_of(chip, k)
        remote(piece, piece, send_f.at[k], recv_d.at[source, k], dev_a).wait_recv()

    barrier = pltpu.get_barrier_semaphore()
    for step in range(1, n):
        pl.semaphore_signal(
            barrier, inc=1, device_id=(sec, lax.rem(me + step, n)), device_id_type=MESH
        )
    for step in range(1, ns):
        pl.semaphore_signal(
            barrier, inc=1, device_id=(lax.rem(sec + step, ns), me), device_id_type=MESH
        )
    own_rows = rows_all.at[pl.ds(pl.multiple_of(chip_o * block, block), block)]
    pairs = (
        (tissue_in, tissue), (w1_in, w1), (x_ref, own_rows), (g1_in, g1), (b1_in, b1),
        (w2_in, w2), (g2_in, g2), (b2_in, b2),
    )
    fetches = [
        pltpu.make_async_copy(src, dst, local_sem.at[i]) for i, (src, dst) in enumerate(pairs)
    ]
    for fetch in fetches:
        fetch.start()
    pl.semaphore_wait(barrier, n - 1 + ns - 1)
    start_own(0)
    start_own(1)
    for fetch in fetches:
        fetch.wait()

    def tile_sums(t, carry):
        total, squares, count = carry
        weight = tissue[0, me * tiles_here + t].astype(jnp.float32)
        start = pl.multiple_of(chip_o * block + t * pixels, 16)
        first = jnp.dot(
            rows_all[pl.ds(start, pixels), :], w1[...], preferred_element_type=jnp.float32
        )
        total += weight * jnp.sum(first, axis=0, keepdims=True)
        squares += weight * jnp.sum(first * first, axis=0, keepdims=True)
        return total, squares, count + weight * pixels

    wide = w1.shape[1]
    zero = jnp.zeros((1, wide), jnp.float32)
    total, squares, count = lax.fori_loop(0, tiles_here, tile_sums, (zero, zero, zero))
    mine = st1.at[me]
    mine[0:1, :] = total
    mine[1:2, :] = squares
    mine[2:3, :] = count
    mine[3:8, :] = jnp.zeros((5, wide), jnp.float32)

    def exchange(buf, slot, count_of, send, recv, device_of):
        copies = []
        for step in range(1, count_of):
            other = lax.rem(slot + step, count_of)
            copy = pltpu.make_async_remote_copy(
                src_ref=buf.at[slot], dst_ref=buf.at[slot],
                send_sem=send.at[step], recv_sem=recv.at[slot],
                device_id=device_of(other), device_id_type=MESH,
            )
            copy.start()
            copies.append((copy, other))
        return copies

    def collect(buf, copies, recv, send, device_of):
        for copy, other in copies:
            copy.wait_send()
        for step, (copy, other) in enumerate(copies):
            pltpu.make_async_remote_copy(
                src_ref=buf.at[other], dst_ref=buf.at[other],
                send_sem=send.at[step + 1], recv_sem=recv.at[other],
                device_id=device_of(other), device_id_type=MESH,
            ).wait_recv()

    def in_space(other):
        return (sec, other)

    def in_section(other):
        return (other, me)

    copies = exchange(st1, me, n, st1_send, st1_recv, in_space)
    lax.fori_loop(2, units, lambda k, c: (start_own(k), c)[1], 0)
    collect(st1, copies, st1_recv, st1_send, in_space)
    st2[sec] = jnp.sum(st1[...], axis=0)
    copies = exchange(st2, sec, ns, st2_send, st2_recv, in_section)
    collect(st2, copies, st2_recv, st2_send, in_section)
    sums = jnp.sum(st2[...], axis=0)
    count = sums[2:3, :]
    mean = sums[0:1, :] / count
    var = sums[1:2, :] / count - mean * mean
    scale = g1[...] * lax.rsqrt(var + EPS)
    stats1_ref[0:1, :] = mean
    stats1_ref[1:2, :] = var
    stats1_ref[2:8, :] = jnp.zeros((6, wide), jnp.float32)
    coef[0:1, :] = scale
    coef[1:2, :] = b1[...] - mean * scale
    coef[2:3, :] = count

    acc[...] = jnp.zeros_like(acc)

    def activate(group, chip, k):
        rows = rows_of(chip, k)[...]
        first = jnp.dot(rows, w1[...], preferred_element_type=jnp.float32)
        act = jnp.maximum(first * coef[0:1, :] + coef[1:2, :], 0.0)
        acts_of(chip, core, k)[...] = act.astype(jnp.bfloat16)
        relay(group, chip, core, k).start()

    def compute(chip, j):
        base = chip * (2 * block) + j * chunk
        act = acts[pl.ds(pl.multiple_of(base, chunk), chunk), :]
        second = jnp.dot(act, w2[...], preferred_element_type=jnp.float32).T
        lane = lax.broadcasted_iota(jnp.int32, (1, chunk), 1)
        tile = (j * chunk) // pixels
        mask = jnp.zeros((1, chunk), jnp.float32)
        for i in range(chunk // pixels + 2):
            at = tile + i
            held = tissue[0, chip * tiles_chip + lax.rem(at, tiles_chip)].astype(jnp.float32)
            low = at * pixels - j * chunk
            mask = jnp.where((lane >= low) & (lane < low + pixels), held, mask)
        kept = second * mask
        square = kept * second
        part = acc[0]
        part2 = acc[1]
        for i in range(chunk // 128):
            part += kept[:, i * 128:(i + 1) * 128]
            part2 += square[:, i * 128:(i + 1) * 128]
        acc[0] = part
        acc[1] = part2
        second_ref[:, pl.ds(pl.multiple_of(base, chunk), chunk)] = second

    def each_unit(m, fn):
        fn(2 * m)

        @pl.when(m < macros - 1)
        def _():
            fn(2 * m + 1)

    def finish(group, chip, m):
        each_unit(m, lambda k: relay(group, chip, 1 - core, k).wait_recv())
        compute(chip, m)

        @pl.when(m < macros - 1)
        def _():
            compute(chip, m + macros)

    def side(s):
        chip = chip_at(lax.rem(core + s, 2), lax.rem(1 - core + s, 2))
        return 1 + lax.rem(core + 1 + s, 2), chip

    def finish_sides(m):
        def one(s, c):
            finish(*side(s), m)
            return c

        lax.fori_loop(0, 2, one, 0)

    last = macros - 1

    def own_step(m, c):
        each_unit(m, lambda k: activate(0, chip_o, k))

        @pl.when(m > 0)
        def _():
            finish(0, chip_o, m - 1)

        return c

    def side_step(m, c):
        def from_b(k):
            arrived(0, chip_b, k)
            forward(k).start()

        def from_a(k):
            arrived(1, chip_a, k)

        each_unit(m, from_b)
        each_unit(m, from_a)

        def one(s, c):
            group, chip = side(s)
            each_unit(m, lambda k: activate(group, chip, k))
            return c

        lax.fori_loop(0, 2, one, 0)

        @pl.when(m == 0)
        def _():
            finish(0, chip_o, last)

        @pl.when(m > 0)
        def _():
            finish_sides(m - 1)

        return c

    def last_step(m, c):
        def from_d(k):
            arrived(2, chip_d, k)
            activate(3, chip_d, k)

        @pl.when(m == 0)
        def _():
            finish_sides(last)

        each_unit(m, from_d)

        @pl.when(m < last)
        def _():
            compute(chip_d, m + macros * core)

        each_unit(m, lambda k: relay(3, chip_d, 1 - core, k).wait_recv())

        @pl.when(m < last)
        def _():
            compute(chip_d, m + macros * (1 - core))

        return c

    lax.fori_loop(0, macros, own_step, 0)
    lax.fori_loop(0, macros, side_step, 0)
    lax.fori_loop(0, macros, last_step, 0)
    compute(chip_d, last)

    width = w2.shape[1]
    mine = st3.at[sec]
    mine[0:1, :] = jnp.sum(acc[0].T, axis=0, keepdims=True)
    mine[1:2, :] = jnp.sum(acc[1].T, axis=0, keepdims=True)
    mine[2:8, :] = jnp.zeros((6, width), jnp.float32)
    copies = exchange(st3, sec, ns, st3_send, st3_recv, in_section)

    def drain(k, c):
        for copy in own_copies(k):
            copy.wait_send()
        for group in range(4):
            relay(group, chip_o, core, k).wait_send()
        forward(k).wait_send()
        return c

    lax.fori_loop(0, units, drain, 0)
    collect(st3, copies, st3_recv, st3_send, in_section)
    sums = jnp.sum(st3[...], axis=0)
    count = coef[2:3, 0:width]
    mean = sums[0:1, :] / count
    var = sums[1:2, :] / count - mean * mean
    scale = g2[pl.ds(me, 1), :] * lax.rsqrt(var + EPS)
    stats2_ref[0:1, :] = mean
    stats2_ref[1:2, :] = var
    stats2_ref[2:3, :] = scale
    stats2_ref[3:4, :] = b2[pl.ds(me, 1), :] - mean * scale
    stats2_ref[4:8, :] = jnp.zeros((4, width), jnp.float32)


def finish_kernel(
    cols, stats1, stats2, second, out, mean1, var1, mean2, var2,
    held, rows1, rows2, sems, stat_sems,
):
    size = stats2.shape[1]
    scale = jnp.broadcast_to(stats2[2:3, :], (size, size)).T
    shift = jnp.broadcast_to(stats2[3:4, :], (size, size)).T
    for i in range(2):
        rows1[i] = stats1[i:i + 1, :]
        rows2[i] = stats2[i:i + 1, :]
    small = [
        pltpu.make_async_copy(src, dst, stat_sems.at[i])
        for i, (src, dst) in enumerate(
            ((rows1.at[0], mean1), (rows1.at[1], var1), (rows2.at[0], mean2), (rows2.at[1], var2))
        )
    ]
    for copy in small:
        copy.start()

    def write(i):
        span = pl.ds(pl.multiple_of(i * cols, cols), cols)
        return pltpu.make_async_copy(held.at[:, span], out.at[:, span], sems.at[i])

    def one(i, c):
        for j in range(cols // size):
            span = pl.ds(pl.multiple_of(i * cols + j * size, size), size)
            values = second[:, span] * scale + shift
            held[:, span] = jnp.maximum(values, 0.0).astype(held.dtype)
        write(i).start()
        return c

    steps = sems.shape[0]
    lax.fori_loop(0, steps, one, 0)
    for copy in small:
        copy.wait()
    lax.fori_loop(0, steps, lambda i, c: (write(i).wait(), c)[1], 0)


def units_of(block):
    for units in range(3, block, 2):
        unit = block // units
        if block % units == 0 and unit <= 512 and unit % 64 == 0:
            return units
    return None


def gather_shards(
    n, ns, units,
    features, tissue, first_weight, first_gain, first_bias, second_weight, second_gain, second_bias,
):
    _, tiles_here, pixels, depth = features.shape
    block = tiles_here * pixels
    unit = block // units
    wide = first_weight.shape[1]
    width = second_weight.shape[1]
    total = n * block
    vmem = pl.BlockSpec(memory_space=pltpu.VMEM)
    hbm = pl.BlockSpec(memory_space=pltpu.HBM)
    dma = pltpu.SemaphoreType.DMA
    second, stats1, stats2 = pl.pallas_call(
        functools.partial(gather_kernel, (n, ns, units, unit, tiles_here, pixels)),
        out_shape=(
            pltpu.VMEM((width, total), jnp.float32),
            pltpu.VMEM((8, wide), jnp.float32),
            pltpu.VMEM((8, width), jnp.float32),
        ),
        in_specs=[hbm] * 8,
        out_specs=(vmem, vmem, vmem),
        scratch_shapes=[
            pltpu.SMEM(tissue.shape, jnp.int32),
            pltpu.VMEM((depth, wide), jnp.bfloat16),
            pltpu.VMEM((1, wide), jnp.float32),
            pltpu.VMEM((1, wide), jnp.float32),
            pltpu.VMEM((wide, width), jnp.bfloat16),
            pltpu.VMEM((n, width), jnp.float32),
            pltpu.VMEM((n, width), jnp.float32),
            pltpu.VMEM((total // 2, depth), jnp.bfloat16),
            pltpu.VMEM((total, wide), jnp.bfloat16),
            pltpu.VMEM((2, width, 128), jnp.float32),
            pltpu.VMEM((8, wide), jnp.float32),
            pltpu.VMEM((n, 8, wide), jnp.float32),
            pltpu.VMEM((ns, 8, wide), jnp.float32),
            pltpu.VMEM((ns, 8, width), jnp.float32),
            dma((8,)),
            dma((units,)),
            dma((units,)),
            dma((4, units)),
            dma((units,)),
            dma((3, units)),
            dma((4, units)),
            dma((n,)),
            dma((n,)),
            dma((ns,)),
            dma((ns,)),
            dma((ns,)),
            dma((ns,)),
        ],
        compiler_params=pltpu.CompilerParams(
            collective_id=0, has_side_effects=True, vmem_limit_bytes=VMEM_ASKED
        ),
        cost_estimate=pl.CostEstimate(
            flops=2 * total * wide * (depth + width),
            bytes_accessed=2 * block * depth,
            transcendentals=0,
        ),
        name="gather_convs",
    )(
        *(
            pltpu.with_memory_space_constraint(array, pltpu.HBM)
            for array in (
                tissue,
                features.reshape(block, depth),
                first_weight,
                first_gain[None, :],
                first_bias[None, :],
                second_weight,
                second_gain.reshape(n, width),
                second_bias.reshape(n, width),
            )
        )
    )
    lanes = total // 128
    steps = next(s for s in range(14, lanes + 1) if lanes % s == 0)
    cols = total // steps
    output, mean1, var1, mean2, var2 = pl.pallas_call(
        functools.partial(finish_kernel, cols),
        out_shape=(
            jax.ShapeDtypeStruct((width, total), jnp.bfloat16),
            jax.ShapeDtypeStruct((1, wide), jnp.float32),
            jax.ShapeDtypeStruct((1, wide), jnp.float32),
            jax.ShapeDtypeStruct((1, width), jnp.float32),
            jax.ShapeDtypeStruct((1, width), jnp.float32),
        ),
        in_specs=[vmem, vmem, vmem],
        out_specs=(hbm,) * 5,
        scratch_shapes=[
            pltpu.VMEM((width, total), jnp.bfloat16),
            pltpu.VMEM((2, 1, wide), jnp.float32),
            pltpu.VMEM((2, 1, width), jnp.float32),
            dma((steps,)),
            dma((4,)),
        ],
        compiler_params=pltpu.CompilerParams(vmem_limit_bytes=VMEM_ASKED // 2),
        name="second_norm",
    )(*(pltpu.with_memory_space_constraint(x, pltpu.VMEM) for x in (stats1, stats2, second)))
    return output[None], mean1[0], var1[0], mean2[0], var2[0]


def solution(mesh):
    n, ns = mesh.shape["space"], mesh.shape["section"]

    def shards(features, *rest):
        block = features.shape[1] * features.shape[2]
        units = units_of(block)
        width = rest[4].shape[1]
        if n == 8 and units is not None and width == 128:
            return gather_shards(n, ns, units, features, *rest)
        return plain_shards(features, *rest)

    in_specs = (
        P("section", "space", None, None),
        P("section", None),
        P(),
        P(),
        P(),
        P(None, "space"),
        P(),
        P(),
    )
    out_specs = (P("section", "space", None), P(), P(), P("space"), P("space"))
    return jax.shard_map(shards, mesh=mesh, in_specs=in_specs, out_specs=out_specs, check_vma=False)
```
